32 devices in a mesh: row: 16 (over z, x, core), col: 2 (over y).
Axes of the slice: x: 2, y: 2, z: 4, core: 2. Of those that a mesh axis runs over, the one named last changes fastest.
Arguments:
- x_tiles: bfloat16 [32, 16, 1, 128, 128], P('row', 'col'), may hold values from -0.5390625 to 0.5390625
- x_cols: int32 [32, 16, 1], P('row', 'col'), may hold values from 0 to 1, as said below
- keep_cols: int32 [32, 16, 2], P('row', 'col'), may hold values from 0 to 1, as said below
Outputs:
- square: bfloat16 [32, 16, 2, 128, 128], P('row', 'col')
- purified: bfloat16 [32, 16, 2, 128, 128], P('row', 'col')
The draws below stay inside these ranges and needn't reach their ends.
Inputs may be any that keep to these rules, and one draw needn't show every extreme that they name: `x_cols`: within each block row and column panel the 1 entries are distinct. `keep_cols`: within each block row and column panel the 2 entries are distinct.
All inputs are finite; a program needn't handle non-finite values.
Results may differ from the reference program's by a relative error of at most 0.0049.
Values may be sent and summed in bfloat16 or wider, within the bound.
No kernel may reach another device: no remote copies, remote signals or barrier semaphores. Data moves between devices by JAX's collectives and lax.ppermute only.
A program may use at most 64 MiB of HBM per device.

```python
import jax
import jax.numpy as jnp
from jax import lax

TILE = 128
BR = 2
KP = 1
K2 = 2
NB = 32
NPAN = 16


def draw_x_cols(key, part):
    keys = jax.random.split(jax.random.fold_in(key, 11), NB * NPAN)
    picks = jax.vmap(lambda single: jax.random.permutation(single, BR)[:KP])(keys)
    return picks.reshape(NB, NPAN, KP).astype(jnp.int32)


def draw_keep_cols(key, part):
    keys = jax.random.split(jax.random.fold_in(key, 23), NB * NPAN)
    picks = jax.vmap(lambda single: jax.random.permutation(single, BR)[:K2])(keys)
    return picks.reshape(NB, NPAN, K2).astype(jnp.int32)


def levels(rng, extent, shards, smallest, top_value):
    gain, own = 1.0, jax.random.fold_in(rng, 6)
    for position, blocks in shards:
        heights = jnp.exp(jax.random.uniform(jax.random.fold_in(own, position), (blocks,), jnp.float32, smallest / len(shards), top_value / len(shards)))
        gain = gain * jnp.repeat(heights, extent[position] // blocks).reshape([-1 if axis == position else 1 for axis in range(len(extent))])
    return gain


def noise(stream_key, shape, width, reach, cuts=(), kind=jnp.bfloat16):
    result = width * jax.random.normal(stream_key, shape, jnp.float32)
    if cuts:
        result = result * levels(stream_key, shape, cuts, -0.22, 0.18)
    return jnp.clip(result, -reach, reach).astype(kind)


def setup_inputs(seed: int = 0) -> dict:
    key_of = jax.random.split(jax.random.key(seed), 4)
    return {
        "x_tiles": noise(key_of[0], (NB, NPAN, KP, TILE, TILE), 0.09, 0.5390625, ((0, 16), (1, 2))),
        "x_cols": draw_x_cols(jax.random.fold_in(key_of[3], 71), 0),
        "keep_cols": draw_keep_cols(jax.random.fold_in(key_of[3], 71), 0),
    }


def row_product(a_tiles, a_cols, kept_cols, x_tiles, x_cols):
    panels = a_cols.shape[0]
    rows_b = (jnp.arange(panels, dtype=jnp.int32)[:, None] * BR + a_cols).astype(jnp.int32)
    b_rows = x_tiles[rows_b].astype(jnp.float32)
    b_cols = x_cols[rows_b]
    matched = (b_cols[:, :, :, None, :] == kept_cols[None, None, :, :, None]).astype(jnp.float32)
    selected = jnp.einsum('paqtb,paqbnk->paqtnk', matched, b_rows)
    return jnp.einsum('pamn,paqtnk->qtmk', a_tiles.astype(jnp.float32), selected)


def reference(x_tiles, x_cols, keep_cols):
    indices = jnp.arange(NB, dtype=jnp.int32)

    def square_row(index):
        return row_product(x_tiles[index], x_cols[index], keep_cols[index], x_tiles, x_cols)

    square = lax.map(square_row, indices).astype(jnp.bfloat16)

    def cube_row(index):
        return row_product(square[index], keep_cols[index], keep_cols[index], x_tiles, x_cols)

    cube = lax.map(cube_row, indices)
    purified = (3.0 * square.astype(jnp.float32) - 2.0 * cube).astype(jnp.bfloat16)
    return square, purified
```

```python
import functools

import jax
import jax.numpy as jnp
from jax import lax
from jax.experimental import pallas as pl
from jax.experimental.pallas import tpu as pltpu
from jax.sharding import PartitionSpec as P

CORES = 2
FLAG_ROWS = 16


def chunk_sizes(panels):
    last = max(1, (panels * 3) // 8)
    return (panels - last, last)


def ring_chip(position, chips):
    up = 2 * position
    down = 2 * (chips - 1 - position) + 1
    if isinstance(position, int):
        return up if position < chips // 2 else down
    return jnp.where(position < chips // 2, up, down)


def ring_pairs(rows):
    chips = rows // CORES
    pairs = []
    for position in range(chips):
        for core in range(CORES):
            step = 1 if core == 0 else -1
            source = ring_chip(position, chips) * CORES + core
            target = ring_chip((position + step) % chips, chips) * CORES + core
            pairs.append((source, target))
    return pairs


def slot_of(slab, row, rows):
    chips = rows // CORES

    def place(chip):
        return jnp.where(chip % 2 == 0, chip // 2, chips - 1 - chip // 2)

    core = row % CORES
    step = 1 - 2 * core
    distance = (place(slab // CORES) - place(row // CORES)) * step
    distance = lax.rem(distance + chips, chips)
    return jnp.where(slab % CORES == core, distance, chips + distance)


def slab_of(slot, row, rows):
    chips = rows // CORES
    core = row % CORES
    chip = row // CORES
    place = jnp.where(chip % 2 == 0, chip // 2, chips - 1 - chip // 2)
    step = 1 - 2 * core
    position = lax.rem(place + step * (slot % chips) + chips, chips)
    other = core if slot < chips else 1 - core
    return ring_chip(position, chips) * CORES + other


def expand(payload, count, width, tile, out, row0, col0):
    base = count * tile
    flags = payload[base : base + FLAG_ROWS, :]
    per_row = count // width
    for local in range(width):
        for panel in range(per_row):
            index = local * per_row + panel
            block = payload[index * tile : (index + 1) * tile, :]
            right = block * flags[index : index + 1, :]
            left = block - right
            rows = slice(row0 + local * tile, row0 + (local + 1) * tile)
            column = col0 + panel * 2 * tile
            out[rows, column : column + tile] = left
            out[rows, column + tile : column + 2 * tile] = right


def pack_kernel(sizes, cols_ref, x_ref, *outs):
    width, panels, tile = x_ref.shape[0], x_ref.shape[1], x_ref.shape[-1]
    first = 0
    for size, out in zip(sizes, outs):
        row_ids = lax.broadcasted_iota(jnp.int32, (FLAG_ROWS, tile), 0)
        flags = jnp.zeros((FLAG_ROWS, tile), jnp.float32)
        for local in range(width):
            for panel in range(size):
                index = local * size + panel
                out[index * tile : (index + 1) * tile, :] = x_ref[local, first + panel, 0]
                flag = cols_ref[local, first + panel].astype(jnp.float32)
                flags = jnp.where(row_ids == index, flag, flags)
        base = width * size * tile
        out[base : base + FLAG_ROWS, :] = flags.astype(jnp.bfloat16)
        first += size


def left_kernel(sizes, rows, groups, width, tile, *refs):
    out = refs[-1]
    dense = width * tile
    row, mine = lax.axis_index("row"), lax.axis_index("col")
    panels = sum(sizes)
    index = 0
    for shift in range(groups):
        group = lax.rem(mine - shift + groups, groups)
        first = 0
        for size in sizes:
            payload = refs[index]
            index += 1
            base = width * size * tile
            flags = payload[base : base + FLAG_ROWS, :]
            for panel in range(size):
                slot = slot_of(group * panels + first + panel, row, rows)
                for local in range(width):
                    where = local * size + panel
                    block = payload[where * tile : (where + 1) * tile, :]
                    right = block * flags[where : where + 1, :]
                    part = slice(local * tile, (local + 1) * tile)
                    start = pl.multiple_of(slot * dense, dense)
                    out[part, pl.ds(start, tile)] = block - right
                    out[part, pl.ds(start + tile, tile)] = right
            first += size


def square_kernel(size, width, tile, left_ref, *refs):
    pieces, out, right = refs[:-2], refs[-2], refs[-1]
    dense = width * tile
    for slot, piece in enumerate(pieces):
        expand(piece, width * size, width, tile, right, slot * dense, 0)
    out[...] = jnp.dot(
        left_ref[...], right[...], preferred_element_type=jnp.float32
    ).astype(out.dtype)


def place_panels(source, size, first, group, panels, row, rows, dense, out):
    for panel in range(size):
        slot = slot_of(group * panels + first + panel, row, rows)
        out[:, pl.ds(pl.multiple_of(slot * dense, dense), dense)] = source[
            :, panel * dense : (panel + 1) * dense
        ]


def add_slots(pieces, sizes, width, tile, wanted, squares, right, acc):
    dense = width * tile
    for slot, parts in enumerate(pieces):

        @pl.when(wanted(slot))
        def _(slot=slot, parts=parts):
            column = 0
            for size, part in zip(sizes, parts):
                expand(part, width * size, width, tile, right, 0, column)
                column += size * dense
            acc[...] += jnp.dot(
                squares[:, slot * dense : (slot + 1) * dense],
                right[...],
                preferred_element_type=jnp.float32,
            )


def early(slot, sizes, groups, row, rows, mine):
    panels = sum(sizes)
    slab = slab_of(slot, row, rows)
    return (slab // panels == mine) | (lax.rem(slab, panels) < panels - sizes[-1])


def order(keep, left, right):
    first = keep == 0
    return jnp.where(first, left, right), jnp.where(first, right, left)


def cube_kernel(sizes, rows, groups, width, tile, keep_ref, *refs):
    chunks = len(sizes)
    own = refs[:chunks]
    received = refs[chunks : chunks + (groups - 1) * (chunks - 1)]
    flat = refs[chunks + (groups - 1) * (chunks - 1) : -4]
    acc, square, squares, right = refs[-4:]
    pieces = [flat[i * chunks : (i + 1) * chunks] for i in range(rows)]
    dense = width * tile
    row, mine = lax.axis_index("row"), lax.axis_index("col")
    panels = sum(sizes)
    first = 0
    for size, source in zip(sizes, own):
        place_panels(source, size, first, mine, panels, row, rows, dense, squares)
        for panel in range(size):
            for local in range(width):
                part = slice(local * tile, (local + 1) * tile)
                column = panel * dense
                a, b = order(
                    keep_ref[local, first + panel, 0],
                    source[part, column : column + tile],
                    source[part, column + tile : column + 2 * tile],
                )
                square[local, first + panel, 0] = a
                square[local, first + panel, 1] = b
        first += size
    index = 0
    for shift in range(1, groups):
        group = lax.rem(mine - shift + groups, groups)
        first = 0
        for size in sizes[:-1]:
            place_panels(received[index], size, first, group, panels, row, rows, dense, squares)
            first += size
            index += 1
    acc[...] = jnp.zeros_like(acc)
    wanted = functools.partial(
        early, sizes=sizes, groups=groups, row=row, rows=rows, mine=mine
    )
    add_slots(pieces, sizes, width, tile, wanted, squares, right, acc)


def final_kernel(sizes, rows, groups, width, tile, keep_ref, acc_in, *refs):
    chunks = len(sizes)
    own = refs[:chunks]
    received = refs[chunks : chunks + groups - 1]
    flat = refs[chunks + groups - 1 : -4]
    purified, squares, right, acc = refs[-4:]
    pieces = [flat[i * chunks : (i + 1) * chunks] for i in range(rows)]
    dense = width * tile
    row, mine = lax.axis_index("row"), lax.axis_index("col")
    panels = sum(sizes)
    for shift in range(1, groups):
        group = lax.rem(mine - shift + groups, groups)
        place_panels(
            received[shift - 1],
            sizes[-1],
            panels - sizes[-1],
            group,
            panels,
            row,
            rows,
            dense,
            squares,
        )
    acc[...] = acc_in[...]

    def wanted(slot):
        return jnp.logical_not(early(slot, sizes, groups, row, rows, mine))

    add_slots(pieces, sizes, width, tile, wanted, squares, right, acc)
    first = 0
    for size, source in zip(sizes, own):
        for panel in range(size):
            for local in range(width):
                part = slice(local * tile, (local + 1) * tile)
                column = panel * dense
                target = (first + panel) * dense
                value = 3.0 * source[part, column : column + dense].astype(
                    jnp.float32
                ) - 2.0 * acc[part, target : target + dense]
                value = value.astype(purified.dtype)
                a, b = order(
                    keep_ref[local, first + panel, 0], value[:, :tile], value[:, tile:]
                )
                purified[local, first + panel, 0] = a
                purified[local, first + panel, 1] = b
        first += size


def vmem(count):
    return [pl.BlockSpec(memory_space=pltpu.VMEM)] * count


def smem():
    return pl.BlockSpec(memory_space=pltpu.SMEM)


def params(mib):
    return pltpu.CompilerParams(vmem_limit_bytes=mib * 1024 * 1024)


def shards(rows, groups, x_tiles, x_cols, keep_cols):
    width, panels, tile = x_tiles.shape[0], x_tiles.shape[1], x_tiles.shape[-1]
    dense = width * tile
    sizes = chunk_sizes(panels)
    chips = rows // CORES
    forward = ring_pairs(rows)
    backward = [(target, source) for source, target in forward]
    sibling = [(device, device ^ 1) for device in range(rows)]
    bf16, f32 = jnp.bfloat16, jnp.float32

    def across(value, shift):
        pairs = [(group, (group + shift) % groups) for group in range(groups)]
        return lax.ppermute(value, "col", pairs)

    payloads = pl.pallas_call(
        functools.partial(pack_kernel, sizes),
        out_shape=[
            jax.ShapeDtypeStruct((width * size * tile + FLAG_ROWS, tile), bf16) for size in sizes
        ],
        in_specs=[smem()] + vmem(1),
        out_specs=vmem(len(sizes)),
        name="pack",
    )(x_cols.reshape(width, panels), x_tiles)

    lefts = list(payloads)
    for shift in range(1, groups):
        lefts += [across(payload, shift) for payload in payloads]
    left = pl.pallas_call(
        functools.partial(left_kernel, sizes, rows, groups, width, tile),
        out_shape=jax.ShapeDtypeStruct((dense, rows * dense), bf16),
        in_specs=vmem(len(lefts)),
        out_specs=vmem(1)[0],
        compiler_params=params(16),
        name="left",
    )(*lefts)

    pieces = [[None] * len(sizes) for _ in range(rows)]
    squares, received = [], []
    for chunk, payload in enumerate(payloads):
        size = sizes[chunk]
        mine = [None] * chips
        mine[0] = payload
        ahead = behind = payload
        for hop in range(1, chips // 2 + 1):
            ahead = lax.ppermute(ahead, "row", forward)
            mine[chips - hop] = ahead
            if hop < chips - chips // 2:
                behind = lax.ppermute(behind, "row", backward)
                mine[hop] = behind
        for slot in range(chips):
            pieces[slot][chunk] = mine[slot]
            mirrored = (chips - slot) % chips
            pieces[chips + mirrored][chunk] = lax.ppermute(mine[slot], "row", sibling)
        square = pl.pallas_call(
            functools.partial(square_kernel, size, width, tile),
            out_shape=jax.ShapeDtypeStruct((dense, size * dense), bf16),
            in_specs=vmem(1 + rows),
            out_specs=vmem(1)[0],
            scratch_shapes=[pltpu.VMEM((rows * dense, size * dense), bf16)],
            compiler_params=params(40),
            name="square",
        )(left, *[piece[chunk] for piece in pieces])
        squares.append(square)
        received.append([across(square, shift) for shift in range(1, groups)])

    flat = [part for piece in pieces for part in piece]
    already = [part[shift] for shift in range(groups - 1) for part in received[:-1]]
    acc, square_out = pl.pallas_call(
        functools.partial(cube_kernel, sizes, rows, groups, width, tile),
        out_shape=[
            jax.ShapeDtypeStruct((dense, panels * dense), f32),
            jax.ShapeDtypeStruct((width, panels, 2, tile, tile), bf16),
        ],
        in_specs=[smem()] + vmem(len(squares) + len(already) + len(flat)),
        out_specs=vmem(2),
        scratch_shapes=[
            pltpu.VMEM((dense, rows * dense), bf16),
            pltpu.VMEM((dense, panels * dense), bf16),
        ],
        compiler_params=params(40),
        name="cube",
    )(keep_cols, *squares, *already, *flat)

    purified = pl.pallas_call(
        functools.partial(final_kernel, sizes, rows, groups, width, tile),
        out_shape=jax.ShapeDtypeStruct((width, panels, 2, tile, tile), bf16),
        in_specs=[smem()] + vmem(1 + len(squares) + groups - 1 + len(flat)),
        out_specs=vmem(1)[0],
        scratch_shapes=[
            pltpu.VMEM((dense, rows * dense), bf16),
            pltpu.VMEM((dense, panels * dense), bf16),
            pltpu.VMEM((dense, panels * dense), f32),
        ],
        compiler_params=params(40),
        name="final",
    )(keep_cols, acc, *squares, *received[-1], *flat)
    return (square_out, purified)


def solution(mesh):
    in_specs = (P("row", "col", None, None, None), P("row", "col", None), P("row", "col", None))
    out_specs = (P("row", "col", None, None, None), P("row", "col", None, None, None))
    body = functools.partial(shards, mesh.shape["row"], mesh.shape["col"])
    return jax.shard_map(body, mesh=mesh, in_specs=in_specs, out_specs=out_specs, check_vma=False)
```

```python
import functools

import jax
import jax.numpy as jnp
from jax import lax
from jax.experimental import pallas as pl
from jax.experimental.pallas import tpu as pltpu
from jax.sharding import PartitionSpec as P

CORES = 2
FLAG_ROWS = 16


def chunk_sizes(panels):
    last = max(1, (panels * 3) // 8)
    return (panels - last, last)


def hop_groups(chips):
    last = chips // 2
    return ((0, 1), tuple(range(2, last)), (last,))


def ring_chip(position, chips):
    up = 2 * position
    down = 2 * (chips - 1 - position) + 1
    if isinstance(position, int):
        return up if position < chips // 2 else down
    return jnp.where(position < chips // 2, up, down)


def ring_place(chip, chips):
    return jnp.where(chip % 2 == 0, chip // 2, chips - 1 - chip // 2)


def ring_pairs(rows):
    chips = rows // CORES
    pairs = []
    for position in range(chips):
        for core in range(CORES):
            step = 1 if core == 0 else -1
            source = ring_chip(position, chips) * CORES + core
            target = ring_chip((position + step) % chips, chips) * CORES + core
            pairs.append((source, target))
    return pairs


def hop_slabs(hop, chips):
    return 2 if hop == 0 or 2 * hop == chips else 4


def slot_of(slab, row, rows):
    chips = rows // CORES
    core = row % CORES
    other = jnp.where(slab % CORES == core, 0, 1)
    step = (1 - 2 * core) * (2 * other - 1)
    distance = (ring_place(slab // CORES, chips) - ring_place(row // CORES, chips)) * step
    hop = lax.rem(distance + chips, chips)
    near = 2 + 4 * (hop - 1)
    far = 2 + 4 * (chips - hop - 1) + 2
    return jnp.where(hop == 0, 0, jnp.where(hop <= chips // 2, near, far)) + other


def slab_of(slot, row, rows):
    chips = rows // CORES
    core = row % CORES
    other = slot % 2
    hop = 0 if slot < 2 else (slot - 2) // 4 + 1
    if slot >= 2 and (slot - 2) % 4 >= 2:
        hop = chips - hop
    step = (1 - 2 * core) * (2 * other - 1)
    position = lax.rem(ring_place(row // CORES, chips) + step * hop + chips, chips)
    return ring_chip(position, chips) * CORES + (1 - core if other else core)


def lane_flags(values, rows, size, first, lanes):
    width, panels = values.shape
    row = lax.broadcasted_iota(jnp.int32, (rows, panels), 0)
    lane = lax.broadcasted_iota(jnp.int32, (rows, panels), 1)
    total = jnp.zeros((rows, 1), jnp.int32)
    for local in range(width):
        start = local * size
        here = (row >= start) & (row < start + size) & (lane == first + row - start)
        picked = jnp.where(here, jnp.broadcast_to(values[local : local + 1, :], here.shape), 0)
        total += jnp.sum(picked, axis=1, keepdims=True)
    return jnp.broadcast_to(total.astype(jnp.float32), (rows, lanes))


def pack_kernel(size, first, cols_ref, x_ref, *refs):
    out = refs[-1]
    width, tile = x_ref.shape[0], x_ref.shape[-1]
    for local in range(width):
        for panel in range(size):
            index = local * size + panel
            out[index * tile : (index + 1) * tile, :] = x_ref[local, first + panel, 0]
    base = width * size * tile
    flags = lane_flags(cols_ref[...], FLAG_ROWS, size, first, tile)
    out[base : base + FLAG_ROWS, :] = flags.astype(jnp.bfloat16)


def halves(payload, flags, index, tile):
    block = payload[index * tile : (index + 1) * tile, :]
    right = block * flags[index : index + 1, :]
    return block - right, right


def left_kernel(sizes, rows, groups, width, tile, keep_ref, *refs):
    out, kept = refs[-2:]
    dense = width * tile
    row, mine = lax.axis_index("row"), lax.axis_index("col")
    panels = sum(sizes)
    index = 0
    for shift in range(groups):
        group = lax.rem(mine - shift + groups, groups)
        first = 0
        for size in sizes:
            payload = refs[index]
            index += 1
            base = width * size * tile
            flags = payload[base : base + FLAG_ROWS, :]
            for panel in range(size):
                slot = slot_of(group * panels + first + panel, row, rows)
                start = pl.multiple_of(slot * dense, dense)
                for local in range(width):
                    left, right = halves(payload, flags, local * size + panel, tile)
                    part = slice(local * tile, (local + 1) * tile)
                    out[part, pl.ds(start, tile)] = left
                    out[part, pl.ds(start + tile, tile)] = right
            first += size
    kept[...] = lane_flags(keep_ref[...], kept.shape[0], panels, 0, tile)


def square_kernel(size, width, tile, start, count, first, *refs):
    left_ref, pieces = refs[0], refs[1 : 1 + count]
    out, right = refs[-2:]
    dense = width * tile
    for index, piece in enumerate(pieces):
        base = width * size * tile
        flags = piece[base : base + FLAG_ROWS, :]
        for local in range(width):
            part = slice(index * dense + local * tile, index * dense + (local + 1) * tile)
            for panel in range(size):
                a, b = halves(piece, flags, local * size + panel, tile)
                column = panel * dense
                right[part, column : column + tile] = a
                right[part, column + tile : column + 2 * tile] = b
    total = jnp.dot(
        left_ref[:, start * dense : (start + count) * dense],
        right[...],
        preferred_element_type=jnp.float32,
    )
    if not first:
        total += refs[1 + count][...]
    out[...] = total.astype(out.dtype)


def cube_kernel(sizes, rows, groups, width, tile, spans, kept, *refs):
    chunks = len(sizes)
    dense = width * tile
    panels = sum(sizes)
    own = refs[:chunks]
    received = refs[chunks : chunks + (groups - 1) * (chunks - 1)]
    rights = refs[chunks + (groups - 1) * (chunks - 1) : -4]
    acc, square, later, squares = refs[-4:]
    row, mine = lax.axis_index("row"), lax.axis_index("col")

    def place(source, size, first, group):
        for panel in range(size):
            slot = slot_of(group * panels + first + panel, row, rows)
            value = 0 if source is None else source[:, panel * dense : (panel + 1) * dense]
            value = jnp.zeros((dense, dense), jnp.bfloat16) if source is None else value
            squares[:, pl.ds(pl.multiple_of(slot * dense, dense), dense)] = value

    index = 0
    for shift in range(groups):
        group = lax.rem(mine - shift + groups, groups)
        first = 0
        for chunk, size in enumerate(sizes):
            if shift == 0:
                place(own[chunk], size, first, group)
            elif chunk < chunks - 1:
                place(received[index], size, first, group)
                index += 1
            else:
                place(None, size, first, group)
            first += size

    column = 0
    for chunk, size in enumerate(sizes):
        total = None
        for part, (start, count) in enumerate(spans):
            product = jnp.dot(
                squares[:, start * dense : (start + count) * dense],
                rights[chunk * len(spans) + part][...],
                preferred_element_type=jnp.float32,
            )
            total = product if total is None else total + product
        acc[:, column : column + size * dense] = total
        column += size * dense

    last = sizes[-1]
    for part, (start, count) in enumerate(spans):
        for index in range(count):
            slab = slab_of(start + index, row, rows)
            group, panel = slab // panels, lax.rem(slab, panels)
            shift = lax.rem(mine - group + groups, groups)

            @pl.when((shift > 0) & (panel >= panels - last))
            def _(part=part, index=index, shift=shift, panel=panel):
                where = (shift - 1) * last + panel - (panels - last)
                target = pl.ds(pl.multiple_of(where * dense, dense), dense)
                column = 0
                for chunk, size in enumerate(sizes):
                    later[target, column : column + size * dense] = rights[
                        chunk * len(spans) + part
                    ][index * dense : (index + 1) * dense, :]
                    column += size * dense

    first = 0
    for size, source in zip(sizes, own):
        for panel in range(size):
            for local in range(width):
                part = slice(local * tile, (local + 1) * tile)
                column = panel * dense
                a, b = ordered(
                    kept,
                    local * panels + first + panel,
                    source[part, column : column + dense].astype(jnp.float32),
                    tile,
                )
                square[local, first + panel, 0] = a.astype(square.dtype)
                square[local, first + panel, 1] = b.astype(square.dtype)
        first += size


def ordered(kept, index, value, tile):
    left, right = value[:, :tile], value[:, tile:]
    swap = jnp.broadcast_to(kept[index : index + 1, :] > 0.5, left.shape)
    return jnp.where(swap, right, left), jnp.where(swap, left, right)


def final_kernel(sizes, groups, width, tile, kept, acc, later, *refs):
    chunks = len(sizes)
    own = refs[:chunks]
    received = refs[chunks : chunks + groups - 1]
    purified = refs[-1]
    dense = width * tile
    panels = sum(sizes)
    span = sizes[-1] * dense
    first = 0
    for size, source in zip(sizes, own):
        columns = slice(first * dense, (first + size) * dense)
        total = acc[:, columns]
        for shift in range(groups - 1):
            total += jnp.dot(
                received[shift][...],
                later[shift * span : (shift + 1) * span, columns],
                preferred_element_type=jnp.float32,
            )
        value = 3.0 * source[...].astype(jnp.float32) - 2.0 * total
        for panel in range(size):
            for local in range(width):
                part = value[
                    local * tile : (local + 1) * tile, panel * dense : (panel + 1) * dense
                ]
                a, b = ordered(kept, local * panels + first + panel, part, tile)
                purified[local, first + panel, 0] = a.astype(purified.dtype)
                purified[local, first + panel, 1] = b.astype(purified.dtype)
        first += size


def vmem(count):
    return [pl.BlockSpec(memory_space=pltpu.VMEM)] * count


def anywhere(count):
    return [pl.BlockSpec(memory_space=pl.ANY)] * count


def params(mib):
    return pltpu.CompilerParams(vmem_limit_bytes=mib * 1024 * 1024)


def shards(rows, groups, x_tiles, x_cols, keep_cols):
    width, panels, tile = x_tiles.shape[0], x_tiles.shape[1], x_tiles.shape[-1]
    dense = width * tile
    sizes = chunk_sizes(panels)
    chips = rows // CORES
    forward = ring_pairs(rows)
    backward = [(target, source) for source, target in forward]
    sibling = [(device, device ^ 1) for device in range(rows)]
    bf16, f32 = jnp.bfloat16, jnp.float32

    def across(value, shift):
        pairs = [(group, (group + shift) % groups) for group in range(groups)]
        return lax.ppermute(value, "col", pairs)

    cols = x_cols.reshape(width, panels)
    spans, start = [], 0
    for group in hop_groups(chips):
        count = sum(hop_slabs(hop, chips) for hop in group)
        spans.append((start, count))
        start += count

    def pack(chunk, *after):
        size = sizes[chunk]
        return pl.pallas_call(
            functools.partial(pack_kernel, size, sum(sizes[:chunk])),
            out_shape=jax.ShapeDtypeStruct((width * size * tile + FLAG_ROWS, tile), bf16),
            in_specs=vmem(2) + anywhere(len(after)),
            out_specs=vmem(1)[0],
            compiler_params=params(4),
            name="pack",
        )(cols, x_tiles, *after)

    payloads = [pack(chunk) for chunk in range(len(sizes))]
    lefts = list(payloads)
    for shift in range(1, groups):
        lefts += [across(payload, shift) for payload in payloads]
    kept_rows = -(-width * panels // 8) * 8
    left, kept = pl.pallas_call(
        functools.partial(left_kernel, sizes, rows, groups, width, tile),
        out_shape=[
            jax.ShapeDtypeStruct((dense, rows * dense), bf16),
            jax.ShapeDtypeStruct((kept_rows, tile), f32),
        ],
        in_specs=vmem(1 + len(lefts)),
        out_specs=vmem(2),
        compiler_params=params(4),
        name="left",
    )(keep_cols[:, :, 0], *lefts)

    squares, received, rights = [], [], []
    gate = None
    for chunk, payload in enumerate(payloads):
        size = sizes[chunk]
        if gate is not None:
            payload, gate = lax.optimization_barrier((payload, gate))
        ahead = behind = payload
        total = None
        for group, (start, count) in zip(hop_groups(chips), spans):
            pieces = []
            for hop in group:
                if hop > 0:
                    ahead = lax.ppermute(ahead, "row", forward)
                pieces += [ahead, lax.ppermute(ahead, "row", sibling)]
                if 0 < hop < chips - chips // 2:
                    behind = lax.ppermute(behind, "row", backward)
                    pieces += [behind, lax.ppermute(behind, "row", sibling)]
            last = start + count == rows
            operands = [left] + pieces + ([] if total is None else [total])
            total, right = pl.pallas_call(
                functools.partial(
                    square_kernel, size, width, tile, start, count, total is None
                ),
                out_shape=[
                    jax.ShapeDtypeStruct((dense, size * dense), bf16 if last else f32),
                    jax.ShapeDtypeStruct((count * dense, size * dense), bf16),
                ],
                in_specs=vmem(len(operands)),
                out_specs=vmem(2),
                compiler_params=params(4),
                name="square",
            )(*operands)
            rights.append(right)
            gate = behind
        squares.append(total)
        received.append([across(total, shift) for shift in range(1, groups)])

    already = [part[shift] for shift in range(groups - 1) for part in received[:-1]]
    later_rows = (groups - 1) * sizes[-1] * dense
    acc, square_out, later = pl.pallas_call(
        functools.partial(cube_kernel, sizes, rows, groups, width, tile, spans),
        out_shape=[
            jax.ShapeDtypeStruct((dense, panels * dense), f32),
            jax.ShapeDtypeStruct((width, panels, 2, tile, tile), bf16),
            jax.ShapeDtypeStruct((later_rows, panels * dense), bf16),
        ],
        in_specs=vmem(1 + len(squares) + len(already) + len(rights)),
        out_specs=vmem(3),
        scratch_shapes=[pltpu.VMEM((dense, rows * dense), bf16)],
        compiler_params=params(8),
        name="cube",
    )(kept, *squares, *already, *rights)

    purified = pl.pallas_call(
        functools.partial(final_kernel, sizes, groups, width, tile),
        out_shape=jax.ShapeDtypeStruct((width, panels, 2, tile, tile), bf16),
        in_specs=vmem(3 + len(squares) + groups - 1),
        out_specs=vmem(1)[0],
        compiler_params=params(8),
        name="final",
    )(kept, acc, later, *squares, *received[-1])
    return (square_out, purified)


def solution(mesh):
    in_specs = (P("row", "col", None, None, None), P("row", "col", None), P("row", "col", None))
    out_specs = (P("row", "col", None, None, None), P("row", "col", None, None, None))
    body = functools.partial(shards, mesh.shape["row"], mesh.shape["col"])
    return jax.shard_map(body, mesh=mesh, in_specs=in_specs, out_specs=out_specs, check_vma=False)
```

```python
import functools

import jax
import jax.numpy as jnp
from jax import lax
from jax.experimental import pallas as pl
from jax.experimental.pallas import tpu as pltpu
from jax.sharding import PartitionSpec as P

CORES = 2
FLAG_ROWS = 16


def chunk_sizes(panels):
    last = max(1, panels // 2)
    return (panels - last, last)


def part_sizes(sizes):
    return sizes


def hop_groups(chips, chunk):
    last = chips // 2
    return (tuple(range(last - 1)), (last - 1, last))


def spans_of(chips, chunk):
    spans, start = [], 0
    for group in hop_groups(chips, chunk):
        count = sum(1 if hop == 0 or 2 * hop == chips else 2 for hop in group)
        spans.append((start, count))
        start += count
    return spans


def ring_chip(position, chips):
    up = 2 * position
    down = 2 * (chips - 1 - position) + 1
    if isinstance(position, int):
        return up if position < chips // 2 else down
    return jnp.where(position < chips // 2, up, down)


def ring_place(chip, chips):
    return jnp.where(chip % 2 == 0, chip // 2, chips - 1 - chip // 2)


def ring_pairs(rows):
    chips = rows // CORES
    pairs = []
    for position in range(chips):
        for core in range(CORES):
            step = 1 if core == 0 else -1
            source = ring_chip(position, chips) * CORES + core
            target = ring_chip((position + step) % chips, chips) * CORES + core
            pairs.append((source, target))
    return pairs


def slot_of(slab, row, rows):
    chips = rows // CORES
    core = row % CORES
    other = jnp.where(slab % CORES == core, 0, 1)
    step = (1 - 2 * core) * (2 * other - 1)
    distance = (ring_place(slab // CORES, chips) - ring_place(row // CORES, chips)) * step
    hop = lax.rem(distance + chips, chips)
    near = 2 * hop - 1
    far = 2 * (chips - hop)
    place = jnp.where(hop == 0, 0, jnp.where(hop <= chips // 2, near, far))
    return place + chips * other


def slab_of(slot, row, rows):
    chips = rows // CORES
    core = row % CORES
    other, place = slot // chips, slot % chips
    hop = (place + 1) // 2
    if place > 0 and place % 2 == 0:
        hop = chips - hop
    step = (1 - 2 * core) * (2 * other - 1)
    position = lax.rem(ring_place(row // CORES, chips) + step * hop + chips, chips)
    return ring_chip(position, chips) * CORES + (1 - core if other else core)


def lane_flags(values, rows, size, first, lanes):
    width, panels = values.shape
    row = lax.broadcasted_iota(jnp.int32, (rows, panels), 0)
    lane = lax.broadcasted_iota(jnp.int32, (rows, panels), 1)
    total = jnp.zeros((rows, 1), jnp.int32)
    for local in range(width):
        start = local * size
        here = (row >= start) & (row < start + size) & (lane == first + row - start)
        picked = jnp.where(here, jnp.broadcast_to(values[local : local + 1, :], here.shape), 0)
        total += jnp.sum(picked, axis=1, keepdims=True)
    return jnp.broadcast_to(total.astype(jnp.float32), (rows, lanes))


def pack_kernel(sizes, tile, cols_ref, x_ref, *refs):
    outs, (cols, copied, sems) = refs[:-3], refs[-3:]
    width = x_ref.shape[0]
    columns = pltpu.make_async_copy(cols_ref, cols, copied)
    columns.start()
    copies = []
    first = 0
    for size, out in zip(sizes, outs):
        for local in range(width):
            copy = pltpu.make_async_copy(
                x_ref.at[local, pl.ds(first * tile, size * tile), :],
                out.at[pl.ds(local * size * tile, size * tile), :],
                sems.at[len(copies)],
            )
            copy.start()
            copies.append(copy)
        first += size
    columns.wait()
    first = 0
    for size, out in zip(sizes, outs):
        base = width * size * tile
        flags = lane_flags(cols[...], FLAG_ROWS, size, first, tile)
        out[base : base + FLAG_ROWS, :] = flags.astype(jnp.bfloat16)
        first += size
    for copy in copies:
        copy.wait()


def halves(payload, flags, index, tile):
    block = payload[index * tile : (index + 1) * tile, :]
    right = block * flags[index : index + 1, :]
    return block - right, right


def left_kernel(sizes, rows, groups, width, tile, keep_ref, *refs):
    out, kept = refs[-2:]
    dense = width * tile
    row, mine = lax.axis_index("row"), lax.axis_index("col")
    panels = sum(sizes)
    index = 0
    for shift in range(groups):
        group = lax.rem(mine - shift + groups, groups)
        first = 0
        for size in sizes:
            payload = refs[index]
            index += 1
            base = width * size * tile
            flags = payload[base : base + FLAG_ROWS, :]
            for panel in range(size):
                slot = slot_of(group * panels + first + panel, row, rows)
                start = pl.multiple_of(slot * dense, dense)
                for local in range(width):
                    left, right = halves(payload, flags, local * size + panel, tile)
                    part = slice(local * tile, (local + 1) * tile)
                    out[part, pl.ds(start, tile)] = left
                    out[part, pl.ds(start + tile, tile)] = right
            first += size
    keep = keep_ref[...]
    firsts = jnp.concatenate(
        [keep[local * 2 : local * 2 + 1, :] for local in range(width)], axis=0
    )
    kept[...] = lane_flags(firsts, kept.shape[0], panels, 0, tile)


def square_kernel(size, width, tile, own, pieces, spans, more, parts, *refs):
    refs = list(refs)
    left_ref = refs.pop(0)
    dense = width * tile
    right = refs.pop() if pieces else None
    outs = [refs.pop() for _ in parts][::-1]
    products = []
    if pieces:
        for index in range(pieces):
            piece = refs.pop(0)
            base = width * size * tile
            flags = piece[base : base + FLAG_ROWS, :]
            for local in range(width):
                part = slice(index * dense + local * tile, index * dense + (local + 1) * tile)
                for panel in range(size):
                    a, b = halves(piece, flags, local * size + panel, tile)
                    column = panel * dense
                    right[part, column : column + tile] = a
                    right[part, column + tile : column + 2 * tile] = b
        products.append((own, pieces, right))
    for start, count in spans:
        products.append((start, count, refs.pop(0)))
    total = refs.pop(0)[...] if more else None
    for start, count, other in products:
        product = jnp.dot(
            left_ref[:, start * dense : (start + count) * dense],
            other[...],
            preferred_element_type=jnp.float32,
        )
        total = product if total is None else total + product
    first = 0
    for count, out in zip(parts, outs):
        out[...] = total[:, first * dense : (first + count) * dense].astype(out.dtype)
        first += count


def cube_kernel(sizes, parts, rows, groups, width, tile, spans, kept, *refs):
    dense = width * tile
    panels = sum(sizes)
    early = len(parts) - 1
    own = refs[: len(parts)]
    received = refs[len(parts) : len(parts) + (groups - 1) * early]
    flat = list(refs[len(parts) + (groups - 1) * early : -4])
    rights = [[flat.pop(0) for _ in span] for span in spans]
    acc, square, later, squares = refs[-4:]
    row, mine = lax.axis_index("row"), lax.axis_index("col")

    index = 0
    for shift in range(groups):
        group = lax.rem(mine - shift + groups, groups)
        first = 0
        for part, size in enumerate(parts):
            source = None
            if shift == 0:
                source = own[part]
            elif part < early:
                source = received[index]
                index += 1
            for panel in range(size):
                slot = slot_of(group * panels + first + panel, row, rows)
                where = pl.ds(pl.multiple_of(slot * dense, dense), dense)
                if source is None:
                    squares[:, where] = jnp.zeros((dense, dense), squares.dtype)
                else:
                    squares[:, where] = source[:, panel * dense : (panel + 1) * dense]
            first += size

    column = 0
    for chunk, size in enumerate(sizes):
        total = None
        for (start, count), right in zip(spans[chunk], rights[chunk]):
            product = jnp.dot(
                squares[:, start * dense : (start + count) * dense],
                right[...],
                preferred_element_type=jnp.float32,
            )
            total = product if total is None else total + product
        acc[:, column : column + size * dense] = total
        column += size * dense

    last = parts[-1]
    for position in range(rows):
        slab = slab_of(position, row, rows)
        group, panel = slab // panels, lax.rem(slab, panels)
        shift = lax.rem(mine - group + groups, groups)

        @pl.when((shift > 0) & (panel >= panels - last))
        def _(position=position, shift=shift, panel=panel):
            where = (shift - 1) * last + panel - (panels - last)
            target = pl.ds(pl.multiple_of(where * dense, dense), dense)
            column = 0
            for chunk, size in enumerate(sizes):
                for (start, count), right in zip(spans[chunk], rights[chunk]):
                    if start <= position < start + count:
                        place = (position - start) * dense
                        later[target, column : column + size * dense] = right[
                            place : place + dense, :
                        ]
                column += size * dense

    first = 0
    for size, source in zip(parts, own):
        for panel in range(size):
            for local in range(width):
                part = slice(local * tile, (local + 1) * tile)
                column = panel * dense
                a, b = ordered(
                    kept,
                    local * panels + first + panel,
                    source[part, column : column + dense].astype(jnp.float32),
                    tile,
                )
                square[local, first + panel, 0] = a.astype(square.dtype)
                square[local, first + panel, 1] = b.astype(square.dtype)
        first += size


def ordered(kept, index, value, tile):
    left, right = value[:, :tile], value[:, tile:]
    swap = jnp.broadcast_to(kept[index : index + 1, :] > 0.5, left.shape)
    return jnp.where(swap, right, left), jnp.where(swap, left, right)


def final_kernel(parts, groups, width, tile, kept, acc, later, *refs):
    own = refs[: len(parts)]
    received = refs[len(parts) : len(parts) + groups - 1]
    purified = refs[-1]
    dense = width * tile
    panels = sum(parts)
    span = parts[-1] * dense
    first = 0
    for size, source in zip(parts, own):
        columns = slice(first * dense, (first + size) * dense)
        total = acc[:, columns]
        for shift in range(groups - 1):
            total += jnp.dot(
                received[shift][...],
                later[shift * span : (shift + 1) * span, columns],
                preferred_element_type=jnp.float32,
            )
        value = 3.0 * source[...].astype(jnp.float32) - 2.0 * total
        for panel in range(size):
            for local in range(width):
                part = value[
                    local * tile : (local + 1) * tile, panel * dense : (panel + 1) * dense
                ]
                a, b = ordered(kept, local * panels + first + panel, part, tile)
                purified[local, first + panel, 0] = a.astype(purified.dtype)
                purified[local, first + panel, 1] = b.astype(purified.dtype)
        first += size


def vmem(count):
    return [pl.BlockSpec(memory_space=pltpu.VMEM)] * count


def anywhere(count):
    return [pl.BlockSpec(memory_space=pl.ANY)] * count


def after(value, *others):
    return lax.optimization_barrier((value,) + others)[0] if others else value


def params(mib):
    return pltpu.CompilerParams(vmem_limit_bytes=mib * 1024 * 1024)


def shards(rows, groups, x_tiles, x_cols, keep_cols):
    width, panels, tile = x_tiles.shape[0], x_tiles.shape[1], x_tiles.shape[-1]
    dense = width * tile
    sizes = chunk_sizes(panels)
    parts = part_sizes(sizes)
    chips = rows // CORES
    hops = chips // 2
    forward = ring_pairs(rows)
    backward = [(target, source) for source, target in forward]
    sibling = [(device, device ^ 1) for device in range(rows)]
    bf16, f32 = jnp.bfloat16, jnp.float32

    def across(value, shift):
        pairs = [(group, (group + shift) % groups) for group in range(groups)]
        return lax.ppermute(value, "col", pairs)

    payloads = pl.pallas_call(
        functools.partial(pack_kernel, sizes, tile),
        out_shape=[
            jax.ShapeDtypeStruct((width * size * tile + FLAG_ROWS, tile), bf16) for size in sizes
        ],
        in_specs=anywhere(2),
        out_specs=vmem(len(sizes)),
        scratch_shapes=[
            pltpu.VMEM((width, panels), jnp.int32),
            pltpu.SemaphoreType.DMA,
            pltpu.SemaphoreType.DMA((width * len(sizes),)),
        ],
        compiler_params=params(4),
        name="pack",
    )(x_cols.reshape(width, panels), x_tiles.reshape(width, panels * tile, tile))

    lefts = list(payloads)
    for shift in range(1, groups):
        lefts += [across(payload, shift) for payload in payloads]
    kept_rows = -(-width * panels // 8) * 8
    left, kept = pl.pallas_call(
        functools.partial(left_kernel, sizes, rows, groups, width, tile),
        out_shape=[
            jax.ShapeDtypeStruct((dense, rows * dense), bf16),
            jax.ShapeDtypeStruct((kept_rows, tile), f32),
        ],
        in_specs=vmem(1 + len(lefts)),
        out_specs=vmem(2),
        compiler_params=params(4),
        name="left",
    )(jnp.transpose(keep_cols, (0, 2, 1)).reshape(width * 2, panels), *lefts)

    def square_of(size, own, pieces, swapped, total, outs):
        operands = [left] + pieces + [value for _, value in swapped]
        operands += [] if total is None else [total]
        done = len(outs) > 1 or not pieces
        shapes = [jax.ShapeDtypeStruct((dense, n * dense), bf16 if done else f32) for n in outs]
        if pieces:
            shapes.append(jax.ShapeDtypeStruct((len(pieces) * dense, size * dense), bf16))
        return pl.pallas_call(
            functools.partial(
                square_kernel,
                size,
                width,
                tile,
                own,
                len(pieces),
                [span for span, _ in swapped],
                total is not None,
                outs,
            ),
            out_shape=shapes,
            in_specs=vmem(len(operands)),
            out_specs=vmem(len(shapes)),
            compiler_params=params(4),
            name="square",
        )(*operands)

    both_spans, rights, squares, received = [], [], [], []
    for chunk, payload in enumerate(payloads):
        size = sizes[chunk]
        counts = {True: hops - chunk, False: hops - 1 + chunk}
        moved = {True: [payload], False: [payload]}
        for hop in range(1, hops + 1):
            for ahead in (True, False):
                if hop <= counts[ahead]:
                    pairs = forward if ahead else backward
                    moved[ahead].append(lax.ppermute(moved[ahead][-1], "row", pairs))
        spans = spans_of(chips, chunk)
        sib_spans = [(start + chips, count) for start, count in spans]
        own_rights, sib_rights = [], []
        total, swapped = None, []
        for part, group in enumerate(hop_groups(chips, chunk)):
            pieces = []
            for hop in group:
                if hop == 0:
                    pieces.append(payload)
                    continue
                pieces += [moved[key][hop] for key in (True, False) if hop < len(moved[key])]
            total, right = square_of(size, spans[part][0], pieces, swapped, total, [size])
            own_rights.append(right)
            sib_rights.append(lax.ppermute(right, "row", sibling))
            swapped = [(sib_spans[part], sib_rights[-1])]
        (square,) = square_of(size, None, [], swapped, total, [size])
        rights.append(own_rights + sib_rights)
        both_spans.append(spans + sib_spans)
        squares.append(square)
        received.append([across(square, shift) for shift in range(1, groups)])

    dense_rights = [right for some in rights for right in some]
    already = [part[shift] for shift in range(groups - 1) for part in received[:-1]]
    later_rows = (groups - 1) * parts[-1] * dense
    acc, square_out, later = pl.pallas_call(
        functools.partial(cube_kernel, sizes, parts, rows, groups, width, tile, both_spans),
        out_shape=[
            jax.ShapeDtypeStruct((dense, panels * dense), f32),
            jax.ShapeDtypeStruct((width, panels, 2, tile, tile), bf16),
            jax.ShapeDtypeStruct((later_rows, panels * dense), bf16),
        ],
        in_specs=vmem(1 + len(squares) + len(already) + len(dense_rights)),
        out_specs=vmem(3),
        scratch_shapes=[pltpu.VMEM((dense, rows * dense), bf16)],
        compiler_params=params(8),
        name="cube",
    )(kept, *squares, *already, *dense_rights)

    purified = pl.pallas_call(
        functools.partial(final_kernel, parts, groups, width, tile),
        out_shape=jax.ShapeDtypeStruct((width, panels, 2, tile, tile), bf16),
        in_specs=vmem(3 + len(squares) + groups - 1),
        out_specs=vmem(1)[0],
        compiler_params=params(8),
        name="final",
    )(kept, acc, later, *squares, *received[-1])
    return (square_out, purified)


def solution(mesh):
    in_specs = (P("row", "col", None, None, None), P("row", "col", None), P("row", "col", None))
    out_specs = (P("row", "col", None, None, None), P("row", "col", None, None, None))
    body = functools.partial(shards, mesh.shape["row"], mesh.shape["col"])
    return jax.shard_map(body, mesh=mesh, in_specs=in_specs, out_specs=out_specs, check_vma=False)
```

```python
import functools

import jax
import jax.numpy as jnp
from jax import lax
from jax.experimental import pallas as pl
from jax.experimental.pallas import tpu as pltpu
from jax.sharding import PartitionSpec as P

CORES = 2
FLAG_ROWS = 16


def chunk_sizes(panels):
    last = max(1, panels//2)
    return (panels - last, last)


def hop_groups(chips):
    last = chips // 2
    return ((0, 1), tuple(range(2, last)), (last,))


def spans_of(groups, chips):
    spans, start = [], 0
    for group in groups:
        count = sum(hop_slabs(hop, chips) for hop in group)
        spans.append((start, count))
        start += count
    return spans


def ring_chip(position, chips):
    up = 2 * position
    down = 2 * (chips - 1 - position) + 1
    if isinstance(position, int):
        return up if position < chips // 2 else down
    return jnp.where(position < chips // 2, up, down)


def ring_place(chip, chips):
    return jnp.where(chip % 2 == 0, chip // 2, chips - 1 - chip // 2)


def ring_pairs(rows):
    chips = rows // CORES
    pairs = []
    for position in range(chips):
        for core in range(CORES):
            step = 1 if core == 0 else -1
            source = ring_chip(position, chips) * CORES + core
            target = ring_chip((position + step) % chips, chips) * CORES + core
            pairs.append((source, target))
    return pairs


def hop_slabs(hop, chips):
    return 2 if hop == 0 or 2 * hop == chips else 4


def slot_of(slab, row, rows):
    chips = rows // CORES
    core = row % CORES
    other = jnp.where(slab % CORES == core, 0, 1)
    step = (1 - 2 * core) * (2 * other - 1)
    distance = (ring_place(slab // CORES, chips) - ring_place(row // CORES, chips)) * step
    hop = lax.rem(distance + chips, chips)
    near = 2 + 4 * (hop - 1)
    far = 2 + 4 * (chips - hop - 1) + 2
    return jnp.where(hop == 0, 0, jnp.where(hop <= chips // 2, near, far)) + other


def slab_of(slot, row, rows):
    chips = rows // CORES
    core = row % CORES
    other = slot % 2
    hop = 0 if slot < 2 else (slot - 2) // 4 + 1
    if slot >= 2 and (slot - 2) % 4 >= 2:
        hop = chips - hop
    step = (1 - 2 * core) * (2 * other - 1)
    position = lax.rem(ring_place(row // CORES, chips) + step * hop + chips, chips)
    return ring_chip(position, chips) * CORES + (1 - core if other else core)


def lane_flags(values, rows, size, first, lanes):
    width, panels = values.shape
    row = lax.broadcasted_iota(jnp.int32, (rows, panels), 0)
    lane = lax.broadcasted_iota(jnp.int32, (rows, panels), 1)
    total = jnp.zeros((rows, 1), jnp.int32)
    for local in range(width):
        start = local * size
        here = (row >= start) & (row < start + size) & (lane == first + row - start)
        picked = jnp.where(here, jnp.broadcast_to(values[local : local + 1, :], here.shape), 0)
        total += jnp.sum(picked, axis=1, keepdims=True)
    return jnp.broadcast_to(total.astype(jnp.float32), (rows, lanes))


def pack_kernel(sizes, tile, cols_ref, x_ref, *refs):
    outs, (cols, copied, sems) = refs[:-3], refs[-3:]
    width = x_ref.shape[0]
    columns = pltpu.make_async_copy(cols_ref, cols, copied)
    columns.start()
    copies = []
    first = 0
    for size, out in zip(sizes, outs):
        for local in range(width):
            copy = pltpu.make_async_copy(
                x_ref.at[local, pl.ds(first * tile, size * tile), :],
                out.at[pl.ds(local * size * tile, size * tile), :],
                sems.at[len(copies)],
            )
            copy.start()
            copies.append(copy)
        first += size
    columns.wait()
    first = 0
    for size, out in zip(sizes, outs):
        base = width * size * tile
        flags = lane_flags(cols[...], FLAG_ROWS, size, first, tile)
        out[base : base + FLAG_ROWS, :] = flags.astype(jnp.bfloat16)
        first += size
    for copy in copies:
        copy.wait()


def halves(payload, flags, index, tile):
    block = payload[index * tile : (index + 1) * tile, :]
    right = block * flags[index : index + 1, :]
    return block - right, right


def left_kernel(sizes, rows, groups, width, tile, keep_ref, *refs):
    out, kept = refs[-2:]
    dense = width * tile
    row, mine = lax.axis_index("row"), lax.axis_index("col")
    panels = sum(sizes)
    index = 0
    for shift in range(groups):
        group = lax.rem(mine - shift + groups, groups)
        first = 0
        for size in sizes:
            payload = refs[index]
            index += 1
            base = width * size * tile
            flags = payload[base : base + FLAG_ROWS, :]
            for panel in range(size):
                slot = slot_of(group * panels + first + panel, row, rows)
                start = pl.multiple_of(slot * dense, dense)
                for local in range(width):
                    left, right = halves(payload, flags, local * size + panel, tile)
                    part = slice(local * tile, (local + 1) * tile)
                    out[part, pl.ds(start, tile)] = left
                    out[part, pl.ds(start + tile, tile)] = right
            first += size
    keep = keep_ref[...]
    firsts = jnp.concatenate(
        [keep[local * 2 : local * 2 + 1, :] for local in range(width)], axis=0
    )
    kept[...] = lane_flags(firsts, kept.shape[0], panels, 0, tile)


def square_kernel(size, width, tile, start, count, first, *refs):
    left_ref, pieces = refs[0], refs[1 : 1 + count]
    out, right = refs[-2:]
    dense = width * tile
    for index, piece in enumerate(pieces):
        base = width * size * tile
        flags = piece[base : base + FLAG_ROWS, :]
        for local in range(width):
            part = slice(index * dense + local * tile, index * dense + (local + 1) * tile)
            for panel in range(size):
                a, b = halves(piece, flags, local * size + panel, tile)
                column = panel * dense
                right[part, column : column + tile] = a
                right[part, column + tile : column + 2 * tile] = b
    total = jnp.dot(
        left_ref[:, start * dense : (start + count) * dense],
        right[...],
        preferred_element_type=jnp.float32,
    )
    if not first:
        total += refs[1 + count][...]
    out[...] = total.astype(out.dtype)


def cube_kernel(sizes, rows, groups, width, tile, spans, kept, *refs):
    chunks = len(sizes)
    dense = width * tile
    panels = sum(sizes)
    own = refs[:chunks]
    received = refs[chunks : chunks + (groups - 1) * (chunks - 1)]
    flat = list(refs[chunks + (groups - 1) * (chunks - 1) : -4])
    rights = [[flat.pop(0) for _ in spans[chunk]] for chunk in range(chunks)]
    acc, square, later, squares = refs[-4:]
    row, mine = lax.axis_index("row"), lax.axis_index("col")

    def place(source, size, first, group):
        for panel in range(size):
            slot = slot_of(group * panels + first + panel, row, rows)
            value = 0 if source is None else source[:, panel * dense : (panel + 1) * dense]
            value = jnp.zeros((dense, dense), jnp.bfloat16) if source is None else value
            squares[:, pl.ds(pl.multiple_of(slot * dense, dense), dense)] = value

    index = 0
    for shift in range(groups):
        group = lax.rem(mine - shift + groups, groups)
        first = 0
        for chunk, size in enumerate(sizes):
            if shift == 0:
                place(own[chunk], size, first, group)
            elif chunk < chunks - 1:
                place(received[index], size, first, group)
                index += 1
            else:
                place(None, size, first, group)
            first += size

    column = 0
    for chunk, size in enumerate(sizes):
        total = None
        for part, (start, count) in enumerate(spans[chunk]):
            product = jnp.dot(
                squares[:, start * dense : (start + count) * dense],
                rights[chunk][part][...],
                preferred_element_type=jnp.float32,
            )
            total = product if total is None else total + product
        acc[:, column : column + size * dense] = total
        column += size * dense

    last = sizes[-1]
    for position in range(rows):
        slab = slab_of(position, row, rows)
        group, panel = slab // panels, lax.rem(slab, panels)
        shift = lax.rem(mine - group + groups, groups)

        @pl.when((shift > 0) & (panel >= panels - last))
        def _(position=position, shift=shift, panel=panel):
            where = (shift - 1) * last + panel - (panels - last)
            target = pl.ds(pl.multiple_of(where * dense, dense), dense)
            column = 0
            for chunk, size in enumerate(sizes):
                for part, (start, count) in enumerate(spans[chunk]):
                    if start <= position < start + count:
                        place = (position - start) * dense
                        later[target, column : column + size * dense] = rights[chunk][part][
                            place : place + dense, :
                        ]
                column += size * dense

    first = 0
    for size, source in zip(sizes, own):
        for panel in range(size):
            for local in range(width):
                part = slice(local * tile, (local + 1) * tile)
                column = panel * dense
                a, b = ordered(
                    kept,
                    local * panels + first + panel,
                    source[part, column : column + dense].astype(jnp.float32),
                    tile,
                )
                square[local, first + panel, 0] = a.astype(square.dtype)
                square[local, first + panel, 1] = b.astype(square.dtype)
        first += size


def ordered(kept, index, value, tile):
    left, right = value[:, :tile], value[:, tile:]
    swap = jnp.broadcast_to(kept[index : index + 1, :] > 0.5, left.shape)
    return jnp.where(swap, right, left), jnp.where(swap, left, right)


def final_kernel(sizes, groups, width, tile, kept, acc, later, *refs):
    chunks = len(sizes)
    own = refs[:chunks]
    received = refs[chunks : chunks + groups - 1]
    purified = refs[-1]
    dense = width * tile
    panels = sum(sizes)
    span = sizes[-1] * dense
    first = 0
    for size, source in zip(sizes, own):
        columns = slice(first * dense, (first + size) * dense)
        total = acc[:, columns]
        for shift in range(groups - 1):
            total += jnp.dot(
                received[shift][...],
                later[shift * span : (shift + 1) * span, columns],
                preferred_element_type=jnp.float32,
            )
        value = 3.0 * source[...].astype(jnp.float32) - 2.0 * total
        for panel in range(size):
            for local in range(width):
                part = value[
                    local * tile : (local + 1) * tile, panel * dense : (panel + 1) * dense
                ]
                a, b = ordered(kept, local * panels + first + panel, part, tile)
                purified[local, first + panel, 0] = a.astype(purified.dtype)
                purified[local, first + panel, 1] = b.astype(purified.dtype)
        first += size


def vmem(count):
    return [pl.BlockSpec(memory_space=pltpu.VMEM)] * count


def anywhere(count):
    return [pl.BlockSpec(memory_space=pl.ANY)] * count


def after(value, *others):
    return lax.optimization_barrier((value,) + others)[0] if others else value


def params(mib):
    return pltpu.CompilerParams(vmem_limit_bytes=mib * 1024 * 1024)


def shards(rows, groups, x_tiles, x_cols, keep_cols):
    width, panels, tile = x_tiles.shape[0], x_tiles.shape[1], x_tiles.shape[-1]
    dense = width * tile
    sizes = chunk_sizes(panels)
    chips = rows // CORES
    forward = ring_pairs(rows)
    backward = [(target, source) for source, target in forward]
    sibling = [(device, device ^ 1) for device in range(rows)]
    bf16, f32 = jnp.bfloat16, jnp.float32

    def across(value, shift):
        pairs = [(group, (group + shift) % groups) for group in range(groups)]
        return lax.ppermute(value, "col", pairs)

    cols = x_cols.reshape(width, panels)
    keeps = jnp.transpose(keep_cols, (0, 2, 1)).reshape(width * 2, panels)
    kept_rows = -(-width * panels // 8) * 8
    payloads = pl.pallas_call(
        functools.partial(pack_kernel, sizes, tile),
        out_shape=[
            jax.ShapeDtypeStruct((width * size * tile + FLAG_ROWS, tile), bf16) for size in sizes
        ],
        in_specs=anywhere(2),
        out_specs=vmem(len(sizes)),
        scratch_shapes=[
            pltpu.VMEM((width, panels), jnp.int32),
            pltpu.SemaphoreType.DMA,
            pltpu.SemaphoreType.DMA((width * len(sizes),)),
        ],
        compiler_params=params(4),
        name="pack",
    )(cols, x_tiles.reshape(width, panels * tile, tile))

    def sibling_of(value):
        return lax.ppermute(value, "row", sibling)

    def left_of(lefts):
        return pl.pallas_call(
            functools.partial(left_kernel, sizes, rows, groups, width, tile),
            out_shape=[
                jax.ShapeDtypeStruct((dense, rows * dense), bf16),
                jax.ShapeDtypeStruct((kept_rows, tile), f32),
            ],
            in_specs=vmem(1 + len(lefts)),
            out_specs=vmem(2),
            compiler_params=params(4),
            name="left",
        )(keeps, *lefts)

    def square_of(size, span, left, pieces, total, last):
        start, count = span
        operands = [left] + pieces + ([] if total is None else [total])
        return pl.pallas_call(
            functools.partial(square_kernel, size, width, tile, start, count, total is None),
            out_shape=[
                jax.ShapeDtypeStruct((dense, size * dense), bf16 if last else f32),
                jax.ShapeDtypeStruct((count * dense, size * dense), bf16),
            ],
            in_specs=vmem(len(operands)),
            out_specs=vmem(2),
            compiler_params=params(4),
            name="square",
        )(*operands)

    hops = chips // 2
    lefts = list(payloads)
    for shift in range(1, groups):
        lefts += [across(payload, shift) for payload in payloads]
    left, kept = left_of(lefts)
    groups_of = hop_groups(chips)
    spans = [spans_of(groups_of, chips)] * len(sizes)
    moved = [{True: [payload], False: [payload]} for payload in payloads]
    swaps = [{} for _ in payloads]
    rights = [[] for _ in payloads]
    totals = [[] for _ in payloads]
    gates = {}

    def swap(chunk, hop, *waits):
        for key in (True, False):
            if hop < len(moved[chunk][key]) and (hop > 0 or key):
                value = moved[chunk][key][hop]
                swaps[chunk][hop, key] = sibling_of(after(value, *waits))

    def multiply(chunk, part):
        pieces = []
        for hop in groups_of[part]:
            for key in (True, False):
                if (hop, key) in swaps[chunk]:
                    pieces += [moved[chunk][key][hop], swaps[chunk][hop, key]]
        total, right = square_of(
            sizes[chunk],
            spans[chunk][part],
            left,
            pieces,
            totals[chunk][-1] if totals[chunk] else None,
            part == len(groups_of) - 1,
        )
        totals[chunk].append(total)
        rights[chunk].append(right)

    for hop in range(1, hops + 1):
        if hop == hops:
            for chunk in range(len(sizes)):
                for part in range(1):
                    for past in groups_of[part]:
                        swap(chunk, past)
                    multiply(chunk, part)
                    gates.setdefault(hop, []).append(totals[chunk][-1])
        for chunk in range(len(sizes)):
            for ahead in (True, False):
                if hop == hops and ahead == (chunk == 1):
                    continue
                value = after(moved[chunk][ahead][-1], *gates.get(hop, []))
                moved[chunk][ahead].append(
                    lax.ppermute(value, "row", forward if ahead else backward)
                )
    squares, received = [], []
    for chunk in range(len(sizes)):
        for part in range(1, len(groups_of)):
            for past in groups_of[part]:
                swap(chunk, past)
            if chunk > 0 and part == len(groups_of) - 1:
                totals[chunk][-1] = after(totals[chunk][-1], *received[0])
            multiply(chunk, part)
        squares.append(totals[chunk][-1])
        received.append([across(squares[-1], shift) for shift in range(1, groups)])
    rights = [right for some in rights for right in some]

    already = [part[shift] for shift in range(groups - 1) for part in received[:-1]]
    later_rows = (groups - 1) * sizes[-1] * dense
    acc, square_out, later = pl.pallas_call(
        functools.partial(cube_kernel, sizes, rows, groups, width, tile, spans),
        out_shape=[
            jax.ShapeDtypeStruct((dense, panels * dense), f32),
            jax.ShapeDtypeStruct((width, panels, 2, tile, tile), bf16),
            jax.ShapeDtypeStruct((later_rows, panels * dense), bf16),
        ],
        in_specs=vmem(1 + len(squares) + len(already) + len(rights)),
        out_specs=vmem(3),
        scratch_shapes=[pltpu.VMEM((dense, rows * dense), bf16)],
        compiler_params=params(8),
        name="cube",
    )(kept, *squares, *already, *rights)

    purified = pl.pallas_call(
        functools.partial(final_kernel, sizes, groups, width, tile),
        out_shape=jax.ShapeDtypeStruct((width, panels, 2, tile, tile), bf16),
        in_specs=vmem(3 + len(squares) + groups - 1),
        out_specs=vmem(1)[0],
        compiler_params=params(8),
        name="final",
    )(kept, acc, later, *squares, *received[-1])
    return (square_out, purified)


def solution(mesh):
    in_specs = (P("row", "col", None, None, None), P("row", "col", None), P("row", "col", None))
    out_specs = (P("row", "col", None, None, None), P("row", "col", None, None, None))
    body = functools.partial(shards, mesh.shape["row"], mesh.shape["col"])
    return jax.shard_map(body, mesh=mesh, in_specs=in_specs, out_specs=out_specs, check_vma=False)
```

```python
import functools

import jax
import jax.numpy as jnp
from jax import lax
from jax.experimental import pallas as pl
from jax.experimental.pallas import tpu as pltpu
from jax.sharding import PartitionSpec as P

CORES = 2
FLAG_ROWS = 16


def chunk_sizes(panels):
    last = max(1, panels//2)
    return (panels - last, last)


def hop_groups(chips):
    last = chips // 2
    return ((0, 1), tuple(range(2, last)), (last,))


def spans_of(groups, chips):
    spans, start = [], 0
    for group in groups:
        count = sum(hop_slabs(hop, chips) for hop in group)
        spans.append((start, count))
        start += count
    return spans


def ring_chip(position, chips):
    up = 2 * position
    down = 2 * (chips - 1 - position) + 1
    if isinstance(position, int):
        return up if position < chips // 2 else down
    return jnp.where(position < chips // 2, up, down)


def ring_place(chip, chips):
    return jnp.where(chip % 2 == 0, chip // 2, chips - 1 - chip // 2)


def ring_pairs(rows):
    chips = rows // CORES
    pairs = []
    for position in range(chips):
        for core in range(CORES):
            step = 1 if core == 0 else -1
            source = ring_chip(position, chips) * CORES + core
            target = ring_chip((position + step) % chips, chips) * CORES + core
            pairs.append((source, target))
    return pairs


def hop_slabs(hop, chips):
    return 2 if hop == 0 or 2 * hop == chips else 4


def slot_of(slab, row, rows):
    chips = rows // CORES
    core = row % CORES
    other = jnp.where(slab % CORES == core, 0, 1)
    step = (1 - 2 * core) * (2 * other - 1)
    distance = (ring_place(slab // CORES, chips) - ring_place(row // CORES, chips)) * step
    hop = lax.rem(distance + chips, chips)
    near = 2 + 4 * (hop - 1)
    far = 2 + 4 * (chips - hop - 1) + 2
    return jnp.where(hop == 0, 0, jnp.where(hop <= chips // 2, near, far)) + other


def slab_of(slot, row, rows):
    chips = rows // CORES
    core = row % CORES
    other = slot % 2
    hop = 0 if slot < 2 else (slot - 2) // 4 + 1
    if slot >= 2 and (slot - 2) % 4 >= 2:
        hop = chips - hop
    step = (1 - 2 * core) * (2 * other - 1)
    position = lax.rem(ring_place(row // CORES, chips) + step * hop + chips, chips)
    return ring_chip(position, chips) * CORES + (1 - core if other else core)


def lane_flags(values, rows, size, first, lanes):
    width, panels = values.shape
    row = lax.broadcasted_iota(jnp.int32, (rows, panels), 0)
    lane = lax.broadcasted_iota(jnp.int32, (rows, panels), 1)
    total = jnp.zeros((rows, 1), jnp.int32)
    for local in range(width):
        start = local * size
        here = (row >= start) & (row < start + size) & (lane == first + row - start)
        picked = jnp.where(here, jnp.broadcast_to(values[local : local + 1, :], here.shape), 0)
        total += jnp.sum(picked, axis=1, keepdims=True)
    return jnp.broadcast_to(total.astype(jnp.float32), (rows, lanes))


def pack_kernel(sizes, tile, cols_ref, x_ref, *refs):
    outs, (cols, copied, sems) = refs[:-3], refs[-3:]
    width = x_ref.shape[0]
    columns = pltpu.make_async_copy(cols_ref, cols, copied)
    columns.start()
    copies = []
    first = 0
    for size, out in zip(sizes, outs):
        for local in range(width):
            copy = pltpu.make_async_copy(
                x_ref.at[local, pl.ds(first * tile, size * tile), :],
                out.at[pl.ds(local * size * tile, size * tile), :],
                sems.at[len(copies)],
            )
            copy.start()
            copies.append(copy)
        first += size
    columns.wait()
    first = 0
    for size, out in zip(sizes, outs):
        base = width * size * tile
        flags = lane_flags(cols[...], FLAG_ROWS, size, first, tile)
        out[base : base + FLAG_ROWS, :] = flags.astype(jnp.bfloat16)
        first += size
    for copy in copies:
        copy.wait()


def halves(payload, flags, index, tile):
    block = payload[index * tile : (index + 1) * tile, :]
    right = block * flags[index : index + 1, :]
    return block - right, right


def left_kernel(sizes, rows, groups, width, tile, keep_ref, *refs):
    out, kept = refs[-2:]
    dense = width * tile
    row, mine = lax.axis_index("row"), lax.axis_index("col")
    panels = sum(sizes)
    index = 0
    for shift in range(groups):
        group = lax.rem(mine - shift + groups, groups)
        first = 0
        for size in sizes:
            payload = refs[index]
            index += 1
            base = width * size * tile
            flags = payload[base : base + FLAG_ROWS, :]
            for panel in range(size):
                slot = slot_of(group * panels + first + panel, row, rows)
                start = pl.multiple_of(slot * dense, dense)
                for local in range(width):
                    left, right = halves(payload, flags, local * size + panel, tile)
                    part = slice(local * tile, (local + 1) * tile)
                    out[part, pl.ds(start, tile)] = left
                    out[part, pl.ds(start + tile, tile)] = right
            first += size
    keep = keep_ref[...]
    firsts = jnp.concatenate(
        [keep[local * 2 : local * 2 + 1, :] for local in range(width)], axis=0
    )
    kept[...] = lane_flags(firsts, kept.shape[0], panels, 0, tile)


def square_kernel(size, width, tile, start, count, first, *refs):
    left_ref, pieces = refs[0], refs[1 : 1 + count]
    out, right = refs[-2:]
    dense = width * tile
    for index, piece in enumerate(pieces):
        base = width * size * tile
        flags = piece[base : base + FLAG_ROWS, :]
        for local in range(width):
            part = slice(index * dense + local * tile, index * dense + (local + 1) * tile)
            for panel in range(size):
                a, b = halves(piece, flags, local * size + panel, tile)
                column = panel * dense
                right[part, column : column + tile] = a
                right[part, column + tile : column + 2 * tile] = b
    total = jnp.dot(
        left_ref[:, start * dense : (start + count) * dense],
        right[...],
        preferred_element_type=jnp.float32,
    )
    if not first:
        total += refs[1 + count][...]
    out[...] = total.astype(out.dtype)


def cube_kernel(sizes, rows, groups, width, tile, spans, kept, *refs):
    chunks = len(sizes)
    dense = width * tile
    panels = sum(sizes)
    own = refs[:chunks]
    received = refs[chunks : chunks + (groups - 1) * (chunks - 1)]
    flat = list(refs[chunks + (groups - 1) * (chunks - 1) : -4])
    rights = [[flat.pop(0) for _ in spans[chunk]] for chunk in range(chunks)]
    acc, square, later, squares = refs[-4:]
    row, mine = lax.axis_index("row"), lax.axis_index("col")

    def place(source, size, first, group):
        for panel in range(size):
            slot = slot_of(group * panels + first + panel, row, rows)
            value = 0 if source is None else source[:, panel * dense : (panel + 1) * dense]
            value = jnp.zeros((dense, dense), jnp.bfloat16) if source is None else value
            squares[:, pl.ds(pl.multiple_of(slot * dense, dense), dense)] = value

    index = 0
    for shift in range(groups):
        group = lax.rem(mine - shift + groups, groups)
        first = 0
        for chunk, size in enumerate(sizes):
            if shift == 0:
                place(own[chunk], size, first, group)
            elif chunk < chunks - 1:
                place(received[index], size, first, group)
                index += 1
            else:
                place(None, size, first, group)
            first += size

    column = 0
    for chunk, size in enumerate(sizes):
        total = None
        for part, (start, count) in enumerate(spans[chunk]):
            product = jnp.dot(
                squares[:, start * dense : (start + count) * dense],
                rights[chunk][part][...],
                preferred_element_type=jnp.float32,
            )
            total = product if total is None else total + product
        acc[:, column : column + size * dense] = total
        column += size * dense

    last = sizes[-1]
    for position in range(rows):
        slab = slab_of(position, row, rows)
        group, panel = slab // panels, lax.rem(slab, panels)
        shift = lax.rem(mine - group + groups, groups)

        @pl.when((shift > 0) & (panel >= panels - last))
        def _(position=position, shift=shift, panel=panel):
            where = (shift - 1) * last + panel - (panels - last)
            target = pl.ds(pl.multiple_of(where * dense, dense), dense)
            column = 0
            for chunk, size in enumerate(sizes):
                for part, (start, count) in enumerate(spans[chunk]):
                    if start <= position < start + count:
                        place = (position - start) * dense
                        later[target, column : column + size * dense] = rights[chunk][part][
                            place : place + dense, :
                        ]
                column += size * dense

    first = 0
    for size, source in zip(sizes, own):
        for panel in range(size):
            for local in range(width):
                part = slice(local * tile, (local + 1) * tile)
                column = panel * dense
                a, b = ordered(
                    kept,
                    local * panels + first + panel,
                    source[part, column : column + dense].astype(jnp.float32),
                    tile,
                )
                square[local, first + panel, 0] = a.astype(square.dtype)
                square[local, first + panel, 1] = b.astype(square.dtype)
        first += size


def ordered(kept, index, value, tile):
    left, right = value[:, :tile], value[:, tile:]
    swap = jnp.broadcast_to(kept[index : index + 1, :] > 0.5, left.shape)
    return jnp.where(swap, right, left), jnp.where(swap, left, right)


def final_kernel(sizes, groups, width, tile, kept, acc, later, *refs):
    chunks = len(sizes)
    own = refs[:chunks]
    received = refs[chunks : chunks + groups - 1]
    purified, staged, sems = refs[-3:]
    dense = width * tile
    panels = sum(sizes)
    span = sizes[-1] * dense
    copies = []
    first = 0
    for size, source in zip(sizes, own):
        columns = slice(first * dense, (first + size) * dense)
        total = acc[:, columns]
        for shift in range(groups - 1):
            total += jnp.dot(
                received[shift][...],
                later[shift * span : (shift + 1) * span, columns],
                preferred_element_type=jnp.float32,
            )
        value = 3.0 * source[...].astype(jnp.float32) - 2.0 * total
        for panel in range(size):
            for local in range(width):
                part = value[
                    local * tile : (local + 1) * tile, panel * dense : (panel + 1) * dense
                ]
                a, b = ordered(kept, local * panels + first + panel, part, tile)
                staged[local, first + panel, 0] = a.astype(staged.dtype)
                staged[local, first + panel, 1] = b.astype(staged.dtype)
        for local in range(width):
            where = (local, pl.ds(first, size))
            copies.append(
                pltpu.make_async_copy(staged.at[where], purified.at[where], sems.at[len(copies)])
            )
            copies[-1].start()
        first += size
    for copy in copies:
        copy.wait()


def vmem(count):
    return [pl.BlockSpec(memory_space=pltpu.VMEM)] * count


def anywhere(count):
    return [pl.BlockSpec(memory_space=pl.ANY)] * count


def after(value, *others):
    return lax.optimization_barrier((value,) + others)[0] if others else value


def params(mib):
    return pltpu.CompilerParams(vmem_limit_bytes=mib * 1024 * 1024)


def shards(rows, groups, x_tiles, x_cols, keep_cols):
    width, panels, tile = x_tiles.shape[0], x_tiles.shape[1], x_tiles.shape[-1]
    dense = width * tile
    sizes = chunk_sizes(panels)
    chips = rows // CORES
    forward = ring_pairs(rows)
    backward = [(target, source) for source, target in forward]
    sibling = [(device, device ^ 1) for device in range(rows)]
    bf16, f32 = jnp.bfloat16, jnp.float32

    def across(value, shift):
        pairs = [(group, (group + shift) % groups) for group in range(groups)]
        return lax.ppermute(value, "col", pairs)

    cols = x_cols.reshape(width, panels)
    keeps = jnp.transpose(keep_cols, (0, 2, 1)).reshape(width * 2, panels)
    kept_rows = -(-width * panels // 8) * 8
    payloads = pl.pallas_call(
        functools.partial(pack_kernel, sizes, tile),
        out_shape=[
            jax.ShapeDtypeStruct((width * size * tile + FLAG_ROWS, tile), bf16) for size in sizes
        ],
        in_specs=anywhere(2),
        out_specs=vmem(len(sizes)),
        scratch_shapes=[
            pltpu.VMEM((width, panels), jnp.int32),
            pltpu.SemaphoreType.DMA,
            pltpu.SemaphoreType.DMA((width * len(sizes),)),
        ],
        compiler_params=params(4),
        name="pack",
    )(cols, x_tiles.reshape(width, panels * tile, tile))

    def sibling_of(value):
        return lax.ppermute(value, "row", sibling)

    def left_of(lefts):
        return pl.pallas_call(
            functools.partial(left_kernel, sizes, rows, groups, width, tile),
            out_shape=[
                jax.ShapeDtypeStruct((dense, rows * dense), bf16),
                jax.ShapeDtypeStruct((kept_rows, tile), f32),
            ],
            in_specs=vmem(1 + len(lefts)),
            out_specs=vmem(2),
            compiler_params=params(4),
            name="left",
        )(keeps, *lefts)

    def square_of(size, span, left, pieces, total, last):
        start, count = span
        operands = [left] + pieces + ([] if total is None else [total])
        return pl.pallas_call(
            functools.partial(square_kernel, size, width, tile, start, count, total is None),
            out_shape=[
                jax.ShapeDtypeStruct((dense, size * dense), bf16 if last else f32),
                jax.ShapeDtypeStruct((count * dense, size * dense), bf16),
            ],
            in_specs=vmem(len(operands)),
            out_specs=vmem(2),
            compiler_params=params(4),
            name="square",
        )(*operands)

    hops = chips // 2
    lefts = list(payloads)
    for shift in range(1, groups):
        lefts += [across(payload, shift) for payload in payloads]
    left, kept = left_of(lefts)
    groups_of = hop_groups(chips)
    spans = [spans_of(groups_of, chips)] * len(sizes)
    moved = [{True: [payload], False: [payload]} for payload in payloads]
    swaps = [{} for _ in payloads]
    rights = [[] for _ in payloads]
    totals = [[] for _ in payloads]
    gates = {}

    def swap(chunk, hop, *waits):
        for key in (True, False):
            if hop < len(moved[chunk][key]) and (hop > 0 or key):
                value = moved[chunk][key][hop]
                swaps[chunk][hop, key] = sibling_of(after(value, *waits))

    def multiply(chunk, part):
        pieces = []
        for hop in groups_of[part]:
            for key in (True, False):
                if (hop, key) in swaps[chunk]:
                    pieces += [moved[chunk][key][hop], swaps[chunk][hop, key]]
        total, right = square_of(
            sizes[chunk],
            spans[chunk][part],
            left,
            pieces,
            totals[chunk][-1] if totals[chunk] else None,
            part == len(groups_of) - 1,
        )
        totals[chunk].append(total)
        rights[chunk].append(right)

    for hop in range(1, hops + 1):
        if hop == hops:
            for chunk in range(len(sizes)):
                for part in range(1):
                    for past in groups_of[part]:
                        swap(chunk, past)
                    multiply(chunk, part)
                    gates.setdefault(hop, []).append(totals[chunk][-1])
        for chunk in range(len(sizes)):
            for ahead in (True, False):
                if hop == hops and ahead == (chunk == 1):
                    continue
                if chunk > 0 and hop >= hops - 1:
                    continue
                value = after(moved[chunk][ahead][-1], *gates.get(hop, []))
                moved[chunk][ahead].append(
                    lax.ppermute(value, "row", forward if ahead else backward)
                )
    squares, received = [], []
    for chunk in range(len(sizes)):
        for part in range(1, len(groups_of)):
            for past in groups_of[part]:
                swap(chunk, past)
            multiply(chunk, part)
        squares.append(totals[chunk][-1])
        for hop, ahead in ((hops - 1, True), (hops - 1, False), (hops, False)):
            if chunk == 0:
                waits = gates.get(hop, []) + (squares[:1] if ahead else [])
                value = after(moved[1][ahead][-1], *waits)
                moved[1][ahead].append(
                    lax.ppermute(value, "row", forward if ahead else backward)
                )
        ready = after(squares[-1], *received[0]) if chunk > 0 else squares[-1]
        received.append([across(ready, shift) for shift in range(1, groups)])
    rights = [right for some in rights for right in some]

    already = [part[shift] for shift in range(groups - 1) for part in received[:-1]]
    later_rows = (groups - 1) * sizes[-1] * dense
    acc, square_out, later = pl.pallas_call(
        functools.partial(cube_kernel, sizes, rows, groups, width, tile, spans),
        out_shape=[
            jax.ShapeDtypeStruct((dense, panels * dense), f32),
            jax.ShapeDtypeStruct((width, panels, 2, tile, tile), bf16),
            jax.ShapeDtypeStruct((later_rows, panels * dense), bf16),
        ],
        in_specs=vmem(1 + len(squares) + len(already) + len(rights)),
        out_specs=vmem(3),
        scratch_shapes=[pltpu.VMEM((dense, rows * dense), bf16)],
        compiler_params=params(8),
        name="cube",
    )(kept, *squares, *already, *rights)

    purified = pl.pallas_call(
        functools.partial(final_kernel, sizes, groups, width, tile),
        out_shape=jax.ShapeDtypeStruct((width, panels, 2, tile, tile), bf16),
        in_specs=vmem(3 + len(squares) + groups - 1),
        out_specs=anywhere(1)[0],
        scratch_shapes=[
            pltpu.VMEM((width, panels, 2, tile, tile), bf16),
            pltpu.SemaphoreType.DMA((width * len(sizes),)),
        ],
        compiler_params=params(8),
        name="final",
    )(kept, acc, later, *squares, *received[-1])
    return (square_out, purified)


def solution(mesh):
    in_specs = (P("row", "col", None, None, None), P("row", "col", None), P("row", "col", None))
    out_specs = (P("row", "col", None, None, None), P("row", "col", None, None, None))
    body = functools.partial(shards, mesh.shape["row"], mesh.shape["col"])
    return jax.shard_map(body, mesh=mesh, in_specs=in_specs, out_specs=out_specs, check_vma=False)
```

```python
import functools

import jax
import jax.numpy as jnp
from jax import lax
from jax.experimental import pallas as pl
from jax.experimental.pallas import tpu as pltpu
from jax.sharding import PartitionSpec as P

CORES = 2
FLAG_ROWS = 16


def chunk_sizes(panels):
    last = max(1, panels//2)
    return (panels - last, last)


def hop_groups(chips):
    last = chips // 2
    return ((0, 1), tuple(range(2, last)), (last,))


def spans_of(groups, chips):
    spans, start = [], 0
    for group in groups:
        count = sum(hop_slabs(hop, chips) for hop in group)
        spans.append((start, count))
        start += count
    return spans


def ring_chip(position, chips):
    up = 2 * position
    down = 2 * (chips - 1 - position) + 1
    if isinstance(position, int):
        return up if position < chips // 2 else down
    return jnp.where(position < chips // 2, up, down)


def ring_place(chip, chips):
    return jnp.where(chip % 2 == 0, chip // 2, chips - 1 - chip // 2)


def ring_pairs(rows):
    chips = rows // CORES
    pairs = []
    for position in range(chips):
        for core in range(CORES):
            step = 1 if core == 0 else -1
            source = ring_chip(position, chips) * CORES + core
            target = ring_chip((position + step) % chips, chips) * CORES + core
            pairs.append((source, target))
    return pairs


def hop_slabs(hop, chips):
    return 2 if hop == 0 or 2 * hop == chips else 4


def slot_of(slab, row, rows):
    chips = rows // CORES
    core = row % CORES
    other = jnp.where(slab % CORES == core, 0, 1)
    step = (1 - 2 * core) * (2 * other - 1)
    distance = (ring_place(slab // CORES, chips) - ring_place(row // CORES, chips)) * step
    hop = lax.rem(distance + chips, chips)
    near = 2 + 4 * (hop - 1)
    far = 2 + 4 * (chips - hop - 1) + 2
    return jnp.where(hop == 0, 0, jnp.where(hop <= chips // 2, near, far)) + other


def slab_of(slot, row, rows):
    chips = rows // CORES
    core = row % CORES
    other = slot % 2
    hop = 0 if slot < 2 else (slot - 2) // 4 + 1
    if slot >= 2 and (slot - 2) % 4 >= 2:
        hop = chips - hop
    step = (1 - 2 * core) * (2 * other - 1)
    position = lax.rem(ring_place(row // CORES, chips) + step * hop + chips, chips)
    return ring_chip(position, chips) * CORES + (1 - core if other else core)


def lane_flags(values, rows, size, first, lanes):
    width, panels = values.shape
    row = lax.broadcasted_iota(jnp.int32, (rows, panels), 0)
    lane = lax.broadcasted_iota(jnp.int32, (rows, panels), 1)
    total = jnp.zeros((rows, 1), jnp.int32)
    for local in range(width):
        start = local * size
        here = (row >= start) & (row < start + size) & (lane == first + row - start)
        picked = jnp.where(here, jnp.broadcast_to(values[local : local + 1, :], here.shape), 0)
        total += jnp.sum(picked, axis=1, keepdims=True)
    return jnp.broadcast_to(total.astype(jnp.float32), (rows, lanes))


def pack_kernel(sizes, tile, cols_ref, x_ref, *refs):
    outs, (cols, copied, sems) = refs[:-3], refs[-3:]
    width = x_ref.shape[0]
    columns = pltpu.make_async_copy(cols_ref, cols, copied)
    columns.start()
    copies = []
    first = 0
    for size, out in zip(sizes, outs):
        for local in range(width):
            copy = pltpu.make_async_copy(
                x_ref.at[local, pl.ds(first * tile, size * tile), :],
                out.at[pl.ds(local * size * tile, size * tile), :],
                sems.at[len(copies)],
            )
            copy.start()
            copies.append(copy)
        first += size
    columns.wait()
    first = 0
    for size, out in zip(sizes, outs):
        base = width * size * tile
        flags = lane_flags(cols[...], FLAG_ROWS, size, first, tile)
        out[base : base + FLAG_ROWS, :] = flags.astype(jnp.bfloat16)
        first += size
    for copy in copies:
        copy.wait()


def halves(payload, flags, index, tile):
    block = payload[index * tile : (index + 1) * tile, :]
    right = block * flags[index : index + 1, :]
    return block - right, right


def left_kernel(sizes, rows, groups, width, tile, keep_ref, *refs):
    out, kept = refs[-2:]
    dense = width * tile
    row, mine = lax.axis_index("row"), lax.axis_index("col")
    panels = sum(sizes)
    index = 0
    for shift in range(groups):
        group = lax.rem(mine - shift + groups, groups)
        first = 0
        for size in sizes:
            payload = refs[index]
            index += 1
            base = width * size * tile
            flags = payload[base : base + FLAG_ROWS, :]
            for panel in range(size):
                slot = slot_of(group * panels + first + panel, row, rows)
                start = pl.multiple_of(slot * dense, dense)
                for local in range(width):
                    left, right = halves(payload, flags, local * size + panel, tile)
                    part = slice(local * tile, (local + 1) * tile)
                    out[part, pl.ds(start, tile)] = left
                    out[part, pl.ds(start + tile, tile)] = right
            first += size
    keep = keep_ref[...]
    firsts = jnp.concatenate(
        [keep[local * 2 : local * 2 + 1, :] for local in range(width)], axis=0
    )
    kept[...] = lane_flags(firsts, kept.shape[0], panels, 0, tile)


def square_kernel(size, width, tile, start, count, first, *refs):
    left_ref, pieces = refs[0], refs[1 : 1 + count]
    out, right = refs[-2:]
    dense = width * tile
    for index, piece in enumerate(pieces):
        base = width * size * tile
        flags = piece[base : base + FLAG_ROWS, :]
        for local in range(width):
            part = slice(index * dense + local * tile, index * dense + (local + 1) * tile)
            for panel in range(size):
                a, b = halves(piece, flags, local * size + panel, tile)
                column = panel * dense
                right[part, column : column + tile] = a
                right[part, column + tile : column + 2 * tile] = b
    total = jnp.dot(
        left_ref[:, start * dense : (start + count) * dense],
        right[...],
        preferred_element_type=jnp.float32,
    )
    if not first:
        total += refs[1 + count][...]
    out[...] = total.astype(out.dtype)


def cube_kernel(sizes, rows, groups, width, tile, spans, kept, *refs):
    chunks = len(sizes)
    dense = width * tile
    panels = sum(sizes)
    own = refs[:chunks]
    received = refs[chunks : chunks + (groups - 1) * (chunks - 1)]
    flat = list(refs[chunks + (groups - 1) * (chunks - 1) : -4])
    rights = [[flat.pop(0) for _ in spans[chunk]] for chunk in range(chunks)]
    acc, square, later, squares = refs[-4:]
    row, mine = lax.axis_index("row"), lax.axis_index("col")

    def place(source, size, first, group):
        for panel in range(size):
            slot = slot_of(group * panels + first + panel, row, rows)
            value = 0 if source is None else source[:, panel * dense : (panel + 1) * dense]
            value = jnp.zeros((dense, dense), jnp.bfloat16) if source is None else value
            squares[:, pl.ds(pl.multiple_of(slot * dense, dense), dense)] = value

    index = 0
    for shift in range(groups):
        group = lax.rem(mine - shift + groups, groups)
        first = 0
        for chunk, size in enumerate(sizes):
            if shift == 0:
                place(own[chunk], size, first, group)
            elif chunk < chunks - 1:
                place(received[index], size, first, group)
                index += 1
            else:
                place(None, size, first, group)
            first += size

    column = 0
    for chunk, size in enumerate(sizes):
        total = None
        for part, (start, count) in enumerate(spans[chunk]):
            product = jnp.dot(
                squares[:, start * dense : (start + count) * dense],
                rights[chunk][part][...],
                preferred_element_type=jnp.float32,
            )
            total = product if total is None else total + product
        acc[:, column : column + size * dense] = (
            3.0 * own[chunk][...].astype(jnp.float32) - 2.0 * total
        )
        column += size * dense

    last = sizes[-1]
    for position in range(rows):
        slab = slab_of(position, row, rows)
        group, panel = slab // panels, lax.rem(slab, panels)
        shift = lax.rem(mine - group + groups, groups)

        @pl.when((shift > 0) & (panel >= panels - last))
        def _(position=position, shift=shift, panel=panel):
            where = (shift - 1) * last + panel - (panels - last)
            target = pl.ds(pl.multiple_of(where * dense, dense), dense)
            column = 0
            for chunk, size in enumerate(sizes):
                for part, (start, count) in enumerate(spans[chunk]):
                    if start <= position < start + count:
                        place = (position - start) * dense
                        later[target, column : column + size * dense] = rights[chunk][part][
                            place : place + dense, :
                        ]
                column += size * dense

    first = 0
    for size, source in zip(sizes, own):
        for panel in range(size):
            for local in range(width):
                part = slice(local * tile, (local + 1) * tile)
                column = panel * dense
                a, b = ordered(
                    kept,
                    local * panels + first + panel,
                    source[part, column : column + dense].astype(jnp.float32),
                    tile,
                )
                square[local, first + panel, 0] = a.astype(square.dtype)
                square[local, first + panel, 1] = b.astype(square.dtype)
        first += size


def ordered(kept, index, value, tile):
    left, right = value[:, :tile], value[:, tile:]
    swap = jnp.broadcast_to(kept[index : index + 1, :] > 0.5, left.shape)
    return jnp.where(swap, right, left), jnp.where(swap, left, right)


def final_kernel(sizes, groups, width, tile, kept, base, later, *refs):
    received = refs[: groups - 1]
    purified, staged, sems = refs[-3:]
    dense = width * tile
    panels = sum(sizes)
    span = sizes[-1] * dense
    copies = []
    for first in range(0, panels, 2):
        size = min(2, panels - first)
        columns = slice(first * dense, (first + size) * dense)
        total = None
        for shift in range(groups - 1):
            product = jnp.dot(
                received[shift][...],
                later[shift * span : (shift + 1) * span, columns],
                preferred_element_type=jnp.float32,
            )
            total = product if total is None else total + product
        value = base[:, columns] - 2.0 * total
        for panel in range(size):
            for local in range(width):
                part = value[
                    local * tile : (local + 1) * tile, panel * dense : (panel + 1) * dense
                ]
                a, b = ordered(kept, local * panels + first + panel, part, tile)
                staged[local, first + panel, 0] = a.astype(staged.dtype)
                staged[local, first + panel, 1] = b.astype(staged.dtype)
        for local in range(width):
            where = (local, pl.ds(first, size))
            copies.append(
                pltpu.make_async_copy(staged.at[where], purified.at[where], sems.at[len(copies)])
            )
            copies[-1].start()
    for copy in copies:
        copy.wait()


def vmem(count):
    return [pl.BlockSpec(memory_space=pltpu.VMEM)] * count


def anywhere(count):
    return [pl.BlockSpec(memory_space=pl.ANY)] * count


def after(value, *others):
    return lax.optimization_barrier((value,) + others)[0] if others else value


def params(mib):
    return pltpu.CompilerParams(vmem_limit_bytes=mib * 1024 * 1024)


def shards(rows, groups, x_tiles, x_cols, keep_cols):
    width, panels, tile = x_tiles.shape[0], x_tiles.shape[1], x_tiles.shape[-1]
    dense = width * tile
    sizes = chunk_sizes(panels)
    chips = rows // CORES
    forward = ring_pairs(rows)
    backward = [(target, source) for source, target in forward]
    sibling = [(device, device ^ 1) for device in range(rows)]
    bf16, f32 = jnp.bfloat16, jnp.float32

    def across(value, shift):
        pairs = [(group, (group + shift) % groups) for group in range(groups)]
        return lax.ppermute(value, "col", pairs)

    cols = x_cols.reshape(width, panels)
    keeps = jnp.transpose(keep_cols, (0, 2, 1)).reshape(width * 2, panels)
    kept_rows = -(-width * panels // 8) * 8
    payloads = pl.pallas_call(
        functools.partial(pack_kernel, sizes, tile),
        out_shape=[
            jax.ShapeDtypeStruct((width * size * tile + FLAG_ROWS, tile), bf16) for size in sizes
        ],
        in_specs=anywhere(2),
        out_specs=vmem(len(sizes)),
        scratch_shapes=[
            pltpu.VMEM((width, panels), jnp.int32),
            pltpu.SemaphoreType.DMA,
            pltpu.SemaphoreType.DMA((width * len(sizes),)),
        ],
        compiler_params=params(4),
        name="pack",
    )(cols, x_tiles.reshape(width, panels * tile, tile))

    def sibling_of(value):
        return lax.ppermute(value, "row", sibling)

    def left_of(lefts):
        return pl.pallas_call(
            functools.partial(left_kernel, sizes, rows, groups, width, tile),
            out_shape=[
                jax.ShapeDtypeStruct((dense, rows * dense), bf16),
                jax.ShapeDtypeStruct((kept_rows, tile), f32),
            ],
            in_specs=vmem(1 + len(lefts)),
            out_specs=vmem(2),
            compiler_params=params(4),
            name="left",
        )(keeps, *lefts)

    def square_of(size, span, left, pieces, total, last):
        start, count = span
        operands = [left] + pieces + ([] if total is None else [total])
        return pl.pallas_call(
            functools.partial(square_kernel, size, width, tile, start, count, total is None),
            out_shape=[
                jax.ShapeDtypeStruct((dense, size * dense), bf16 if last else f32),
                jax.ShapeDtypeStruct((count * dense, size * dense), bf16),
            ],
            in_specs=vmem(len(operands)),
            out_specs=vmem(2),
            compiler_params=params(4),
            name="square",
        )(*operands)

    hops = chips // 2
    lefts = list(payloads)
    for shift in range(1, groups):
        lefts += [across(payload, shift) for payload in payloads]
    left, kept = left_of(lefts)
    groups_of = hop_groups(chips)
    spans = [spans_of(groups_of, chips)] * len(sizes)
    moved = [{True: [payload], False: [payload]} for payload in payloads]
    swaps = [{} for _ in payloads]
    rights = [[] for _ in payloads]
    totals = [[] for _ in payloads]
    gates = {}

    def swap(chunk, hop, *waits):
        for key in (True, False):
            if hop < len(moved[chunk][key]) and (hop > 0 or key):
                value = moved[chunk][key][hop]
                swaps[chunk][hop, key] = sibling_of(after(value, *waits))

    def multiply(chunk, part):
        pieces = []
        for hop in groups_of[part]:
            for key in (True, False):
                if (hop, key) in swaps[chunk]:
                    pieces += [moved[chunk][key][hop], swaps[chunk][hop, key]]
        total, right = square_of(
            sizes[chunk],
            spans[chunk][part],
            left,
            pieces,
            totals[chunk][-1] if totals[chunk] else None,
            part == len(groups_of) - 1,
        )
        totals[chunk].append(total)
        rights[chunk].append(right)

    for hop in range(1, hops + 1):
        if hop == hops:
            for chunk in range(len(sizes)):
                for part in range(1):
                    for past in groups_of[part]:
                        swap(chunk, past)
                    multiply(chunk, part)
                    gates.setdefault(hop, []).append(totals[chunk][-1])
        for chunk in range(len(sizes)):
            for ahead in (True, False):
                if hop == hops and ahead == (chunk == 1):
                    continue
                if chunk > 0 and hop >= hops - 1:
                    continue
                value = after(moved[chunk][ahead][-1], *gates.get(hop, []))
                moved[chunk][ahead].append(
                    lax.ppermute(value, "row", forward if ahead else backward)
                )
    squares, received = [], []
    for chunk in range(len(sizes)):
        for part in range(1, len(groups_of)):
            for past in groups_of[part]:
                swap(chunk, past)
            multiply(chunk, part)
        squares.append(totals[chunk][-1])
        for hop, ahead in ((hops - 1, True), (hops - 1, False), (hops, False)):
            if chunk == 0:
                waits = gates.get(hop, []) + (squares[:1] if ahead else [])
                value = after(moved[1][ahead][-1], *waits)
                moved[1][ahead].append(
                    lax.ppermute(value, "row", forward if ahead else backward)
                )
        ready = after(squares[-1], *received[0]) if chunk > 0 else squares[-1]
        received.append([across(ready, shift) for shift in range(1, groups)])
    rights = [right for some in rights for right in some]

    already = [part[shift] for shift in range(groups - 1) for part in received[:-1]]
    later_rows = (groups - 1) * sizes[-1] * dense
    acc, square_out, later = pl.pallas_call(
        functools.partial(cube_kernel, sizes, rows, groups, width, tile, spans),
        out_shape=[
            jax.ShapeDtypeStruct((dense, panels * dense), f32),
            jax.ShapeDtypeStruct((width, panels, 2, tile, tile), bf16),
            jax.ShapeDtypeStruct((later_rows, panels * dense), bf16),
        ],
        in_specs=vmem(1 + len(squares) + len(already) + len(rights)),
        out_specs=vmem(3),
        scratch_shapes=[pltpu.VMEM((dense, rows * dense), bf16)],
        compiler_params=params(8),
        name="cube",
    )(kept, *squares, *already, *rights)

    purified = pl.pallas_call(
        functools.partial(final_kernel, sizes, groups, width, tile),
        out_shape=jax.ShapeDtypeStruct((width, panels, 2, tile, tile), bf16),
        in_specs=vmem(3 + groups - 1),
        out_specs=anywhere(1)[0],
        scratch_shapes=[
            pltpu.VMEM((width, panels, 2, tile, tile), bf16),
            pltpu.SemaphoreType.DMA((width * -(-panels // 2),)),
        ],
        compiler_params=params(8),
        name="final",
    )(kept, acc, later, *received[-1])
    return (square_out, purified)


def solution(mesh):
    in_specs = (P("row", "col", None, None, None), P("row", "col", None), P("row", "col", None))
    out_specs = (P("row", "col", None, None, None), P("row", "col", None, None, None))
    body = functools.partial(shards, mesh.shape["row"], mesh.shape["col"])
    return jax.shard_map(body, mesh=mesh, in_specs=in_specs, out_specs=out_specs, check_vma=False)
```
